32 devices in a mesh: pipe: 4 (over z), ctx: 8 (over y, x, core).
Axes of the slice: x: 2, y: 2, z: 4, core: 2. Of those that a mesh axis runs over, the one named last changes fastest.
Arguments:
- queries: bfloat16 [4, 1024, 4096], P('pipe', 'ctx'), may hold values from -6 to 6
- stash: bfloat16 [4, 1024, 1024], P('pipe', 'ctx'), may hold values from -6 to 6
- grad_out: bfloat16 [4, 1024, 4096], P('pipe', 'ctx'), may hold values from -6 to 6
- lengths: int32 [2], replicated, may hold values from 1 to 513, 1024 in all
Outputs:
- grad_kv: bfloat16 [4, 1024, 1024], P('pipe', 'ctx')
The draws below stay inside these ranges and needn't reach their ends.
Inputs may be any that keep to these rules, and one draw needn't show every extreme that they name: The lengths sum to 1024; one document is exactly 513 long.
All inputs are finite; a program needn't handle non-finite values.
Results may differ from the reference program's by a relative error of at most 0.0059.
Values may be sent and summed in bfloat16 or wider, within the bound.
No kernel may reach another device: no remote copies, remote signals or barrier semaphores. Data moves between devices by JAX's collectives and lax.ppermute only.
A program may use at most 64 MiB of HBM per device.

```python
import math
import jax
import jax.numpy as jnp
import numpy as np
from jax import lax

H = 32
KVH = 4
HD = 128
TOK_DEV = 128
REACH = 5
TOKENS = 1024
SECTIONS = 4
DOCS = 2
MOST = 513
N_PIPE = 4


def draw_pair(key):
    key_q = jax.random.fold_in(key, 101)
    key_k = jax.random.fold_in(key, 202)
    queries = jnp.clip(jax.random.normal(key_q, (SECTIONS, TOKENS, H * HD), jnp.float32), -5.0, 5.0)
    stash = jnp.clip(jax.random.normal(key_k, (SECTIONS, TOKENS, 2 * KVH * HD), jnp.float32), -5.0, 5.0)
    return (queries, stash)


def draw_queries(key, part):
    return draw_pair(key)[0].astype(jnp.bfloat16)


def draw_stash(key, part):
    return draw_pair(key)[1].astype(jnp.bfloat16)


def steps_of(rng, dims, split, least, high):
    level, own = 1.0, jax.random.fold_in(rng, 6)
    for dim, shards_of in split:
        draws = jnp.exp(jax.random.uniform(jax.random.fold_in(own, dim), (shards_of,), jnp.float32, least / len(split), high / len(split)))
        level = level * jnp.repeat(draws, dims[dim] // shards_of).reshape([-1 if axis == dim else 1 for axis in range(len(dims))])
    return level


def split_up(number_of, total, most, slope):
    portions = [(1 << 20) // math.isqrt(grade ** slope) + 1 for grade in range(2, number_of + 1)]
    spare, holding = total - most - (number_of - 1), [1] * (number_of - 1)
    while spare > 0:
        movable = [i for i in range(number_of - 1) if holding[i] < most]
        whole, budget = sum([portions[i] for i in movable]), spare
        for i in movable:
            more = min(most - holding[i], max(1, budget * portions[i] // whole), spare)
            holding[i] = holding[i] + more
            spare = spare - more
    return np.array([most] + holding)


def uneven_parts(stream_key, count, total, limit, slope):
    if count == 2:
        one = jax.random.randint(stream_key, (), max(1, total - limit), min(limit, total - 1) + 1)
        return jnp.stack([one, total - one])
    sizes = jnp.asarray(split_up(count, total, limit, slope), jnp.int32)
    twos = (count - 1) // 2
    giver, taker = sizes[1:1 + 2 * twos:2], sizes[2:2 + 2 * twos:2]
    slack = jnp.minimum(giver - 1, limit - taker)
    passed = jax.random.randint(jax.random.fold_in(stream_key, 1), (twos,), 0, 1 << 20) % (slack + 1)
    sizes = sizes.at[1:1 + 2 * twos:2].set(giver - passed).at[2:2 + 2 * twos:2].set(taker + passed)
    return sizes[jax.random.permutation(jax.random.fold_in(stream_key, 2), count)]


def noise(stream_key, shape, width, most, pieces=(), kind=jnp.bfloat16):
    entries = width * jax.random.normal(stream_key, shape, jnp.float32)
    if pieces:
        entries = entries * steps_of(stream_key, shape, pieces, -0.22, 0.18)
    return jnp.clip(entries, -most, most).astype(kind)


def setup_inputs(seed: int = 0) -> dict:
    keys = jax.random.split(jax.random.key(seed), 5)
    return {
        "queries": draw_queries(jax.random.fold_in(keys[4], 71), 0),
        "stash": draw_stash(jax.random.fold_in(keys[4], 71), 0),
        "grad_out": noise(keys[2], (SECTIONS, TOKENS, H * HD), 1.0, 6.0, ((0, 4), (1, 8))),
        "lengths": uneven_parts(keys[3], DOCS, TOKENS, MOST, 2).astype(jnp.int32),
    }


def segment_of(positions, lengths):
    doc_ends = jnp.cumsum(lengths)
    return jnp.sum((doc_ends[None, :] <= positions[:, None]).astype(jnp.int32), axis=1)


def block_grads(query_block, cotangent, key_block, value_block, query_pos, key_pos, query_seg, key_seg):
    score_scale = HD ** -0.5
    query_wide = query_block.astype(jnp.float32)
    cot_wide = cotangent.astype(jnp.float32)
    key_wide = key_block.astype(jnp.float32)
    value_wide = value_block.astype(jnp.float32)
    scores = jnp.einsum("rhgd,khd->hgrk", query_wide, key_wide) * score_scale
    allowed = (key_seg[None, :] == query_seg[:, None]) & (key_pos[None, :] <= query_pos[:, None]) & (key_pos[None, :] >= 0)
    scores = jnp.where(allowed, scores, -1e30)
    row_top = jnp.max(scores, axis=-1, keepdims=True)
    raw_weights = jnp.exp(scores - row_top)
    weights = raw_weights / jnp.sum(raw_weights, axis=-1, keepdims=True)
    weights16 = weights.astype(jnp.bfloat16).astype(jnp.float32)
    output = jnp.einsum("hgrk,khd->rhgd", weights16, value_wide)
    row_delta = jnp.sum(cot_wide * output, axis=-1)
    dweights = jnp.einsum("rhgd,khd->hgrk", cot_wide, value_wide)
    dscores = weights * (dweights - jnp.transpose(row_delta, (1, 2, 0))[..., None]) * score_scale
    dscores = dscores.astype(jnp.bfloat16).astype(jnp.float32)
    grad_key = jnp.einsum("hgrk,rhgd->khd", dscores, query_wide)
    grad_value = jnp.einsum("hgrk,rhgd->khd", weights16, cot_wide)
    return grad_key, grad_value


def section_grads(section_queries, section_kv, section_cot, lengths):
    blocks = TOKENS // TOK_DEV
    group = H // KVH
    query_all = section_queries.reshape(blocks, TOK_DEV, KVH, group, HD)
    cot_all = section_cot.reshape(blocks, TOK_DEV, KVH, group, HD)
    kv_all = section_kv.reshape(blocks, TOK_DEV, 2, KVH, HD)
    padded = jnp.concatenate([jnp.zeros((REACH - 1, TOK_DEV, 2, KVH, HD), kv_all.dtype), kv_all], axis=0)
    joined = jnp.stack([padded[r:r + blocks] for r in range(REACH)], axis=1).reshape(blocks, REACH * TOK_DEV, 2, KVH, HD)

    def per_block(block_items):
        block_index, query_block, cotangent, kv_block = block_items
        first_row = block_index * TOK_DEV
        key_pos = first_row - (REACH - 1) * TOK_DEV + jnp.arange(REACH * TOK_DEV, dtype=jnp.int32)
        key_seg = segment_of(key_pos, lengths)
        tail = (REACH - 1) * TOK_DEV
        return block_grads(query_block, cotangent, kv_block[:, 0], kv_block[:, 1], key_pos[tail:], key_pos, key_seg[tail:], key_seg)

    grad_key, grad_value = lax.map(per_block, (jnp.arange(blocks, dtype=jnp.int32), query_all, cot_all, joined))
    key_grads = jnp.stack([grad_key, grad_value], axis=2).reshape(blocks, REACH, TOK_DEV, 2, KVH, HD)
    total = jnp.zeros((blocks, TOK_DEV, 2, KVH, HD), jnp.float32)
    for back in range(REACH):
        contrib = key_grads[:, REACH - 1 - back]
        if back > 0:
            contrib = jnp.concatenate([contrib[back:], jnp.zeros_like(contrib[:back])], axis=0)
        total = total + contrib
    return total.astype(jnp.bfloat16).reshape(TOKENS, 2 * KVH * HD)


def reference(queries, stash, grad_out, lengths):
    mirror = jnp.bitwise_xor(jnp.arange(N_PIPE, dtype=jnp.int32), N_PIPE // 2)
    held_kv = stash[mirror]

    def per_section(section_items):
        return section_grads(section_items[0], section_items[1], section_items[2], lengths)

    return lax.map(per_section, (queries, held_kv, grad_out))
```

```python
import functools
import math

import jax
import jax.numpy as jnp
from jax import lax
from jax.experimental import pallas as pl
from jax.experimental.pallas import tpu as pltpu
from jax.sharding import PartitionSpec as P

H = 32
KVH = 4
HD = 128
REACH = 5
GROUP = REACH - 1
SHARE = H // KVH
PARTS = ((0,), (1,), (2,), (3,))
MASKED = -1e30
F32 = jnp.float32
NT = (((1,), (1,)), ((), ()))
NN = (((1,), (0,)), ((), ()))


def rows_from(ref, first, size):
    return ref[pl.ds(pl.multiple_of(first, 16), size), :]


def doc_start(pos, len_ref):
    start = jnp.zeros_like(pos)
    end = jnp.int32(0)
    for doc in range(len_ref.shape[0]):
        end = end + len_ref[doc]
        start = jnp.where(end <= pos, end, start)
    return start


def bias_of(first_key, keys, query_pos, start):
    key_pos = first_key + lax.broadcasted_iota(jnp.int32, (keys, query_pos.shape[1]), 0)
    return jnp.where((key_pos >= start) & (key_pos <= query_pos), 0.0, MASKED)


def weigh(key, value, query, cot, bias, keep):
    scores = lax.dot_general(key, query, NT, preferred_element_type=F32) + bias
    top = jnp.max(scores, axis=0, keepdims=True)
    raw = jnp.exp2((scores - top) * (HD**-0.5 * math.log2(math.e)))
    weights = raw * (keep / jnp.sum(raw, axis=0, keepdims=True))
    dweights = lax.dot_general(value, cot, NT, preferred_element_type=F32)
    delta = jnp.sum(weights * dweights, axis=0, keepdims=True)
    dscores = weights * (dweights - delta)
    return weights.astype(jnp.bfloat16), dscores.astype(jnp.bfloat16)


def part_kernel(heads, rows, halo, *refs):
    (len_ref, q_ref, g_ref, qh_ref, gh_ref, own_ref, one_ref, two_ref, three_ref, *before_refs, after_ref,
     own_out, one_out, two_out, three_out, before_out, after_out, k_buf, v_buf, bias_ref, dk_ref, dv_ref) = refs
    count = len(heads)
    span = GROUP * rows
    me = lax.axis_index("ctx")
    rank = lax.rem(me, GROUP)
    group_first = (me - rank) * rows
    lane = lax.broadcasted_iota(jnp.int32, (1, rows), 1)
    query_pos = me * rows + lane
    start = doc_start(query_pos, len_ref)
    keep = jnp.where(start < group_first - halo, 0.0, 1.0)
    bias_ref[...] = bias_of(group_first - halo, halo + span, query_pos, start)
    keep2 = jnp.concatenate([keep, keep], axis=1)

    for at, head in enumerate(heads):
        k_cols, v_cols = pl.ds(at * HD, HD), pl.ds((count + at) * HD, HD)
        for step, ref in enumerate((own_ref, one_ref, two_ref, three_ref)):
            row = pl.multiple_of(halo + (rank ^ step) * rows, 16)
            k_buf[pl.ds(row, rows), :] = ref[:, k_cols]
            v_buf[pl.ds(row, rows), :] = ref[:, v_cols]
        all_k, all_v = pl.ds(head * HD, HD), pl.ds((KVH + head) * HD, HD)
        k_buf[:halo, :] = sum(ref[:, all_k] for ref in before_refs)
        v_buf[:halo, :] = sum(ref[:, all_v] for ref in before_refs)
        k_buf[halo + span :, :] = after_ref[:, all_k]
        v_buf[halo + span :, :] = after_ref[:, all_v]
        dk_ref[...] = jnp.zeros_like(dk_ref)
        dv_ref[...] = jnp.zeros_like(dv_ref)

        for case in range(GROUP):

            @pl.when(rank == case)
            def _():
                keys = halo + (case + 1) * rows

                def pair(index, carry):
                    col = at * SHARE * HD + index * 2 * HD
                    query = jnp.concatenate([q_ref[0, :, pl.ds(col + HD * i, HD)] for i in range(2)], axis=0)
                    cot = jnp.concatenate([g_ref[0, :, pl.ds(col + HD * i, HD)] for i in range(2)], axis=0)
                    bias = bias_ref[:keys, :]
                    weights, dscores = weigh(
                        k_buf[:keys, :], v_buf[:keys, :], query, cot, jnp.concatenate([bias, bias], axis=1), keep2
                    )
                    dv_ref[:keys, :] += lax.dot_general(weights, cot, NN, preferred_element_type=F32)
                    dk_ref[:keys, :] += lax.dot_general(dscores, query, NN, preferred_element_type=F32)
                    return carry

                lax.fori_loop(0, SHARE // 2, pair, 0)

        @pl.when(rank == 0)
        def _():
            wide = SHARE * halo
            next_pos = group_first + span + lax.rem(lax.broadcasted_iota(jnp.int32, (1, wide), 1), halo)
            next_start = doc_start(next_pos, len_ref)
            next_keep = jnp.where(next_start < group_first + span - halo, 1.0, 0.0)
            query = jnp.concatenate([qh_ref[:, pl.ds((at * SHARE + i) * HD, HD)] for i in range(SHARE)], axis=0)
            cot = jnp.concatenate([gh_ref[:, pl.ds((at * SHARE + i) * HD, HD)] for i in range(SHARE)], axis=0)
            weights, dscores = weigh(
                k_buf[halo:, :], v_buf[halo:, :], query, cot,
                bias_of(group_first, span + halo, next_pos, next_start), next_keep,
            )
            dv_ref[halo:, :] += lax.dot_general(weights, cot, NN, preferred_element_type=F32)
            dk_ref[halo:, :] += lax.dot_general(dscores, query, NN, preferred_element_type=F32)

        scale = HD**-0.5
        for step, ref in enumerate((own_out, one_out, two_out, three_out)):
            row = halo + (rank ^ step) * rows
            ref[:, k_cols] = (rows_from(dk_ref, row, rows) * scale).astype(ref.dtype)
            ref[:, v_cols] = rows_from(dv_ref, row, rows).astype(ref.dtype)
        for ref, row in ((before_out, 0), (after_out, halo + span)):
            ref[:, k_cols] = (dk_ref[row : row + halo, :] * scale).astype(ref.dtype)
            ref[:, v_cols] = dv_ref[row : row + halo, :].astype(ref.dtype)


def whole_block(shape):
    return pl.BlockSpec(shape, lambda i: (0,) * len(shape))


def part_grads(heads, halo, lengths, queries, grad_out, next_q, next_g, pieces, before, after):
    rows = queries.shape[1]
    count = len(heads)
    assert list(heads) == list(range(heads[0], heads[0] + count)) and heads[0] % count == 0
    wide = count * SHARE * HD
    nth = heads[0] // count
    kv = 2 * count * HD
    keys = halo + GROUP * rows + halo
    q_spec = pl.BlockSpec((1, rows, wide), lambda i: (0, 0, nth))
    h_spec = pl.BlockSpec((halo, wide), lambda i: (0, nth))
    out = [jax.ShapeDtypeStruct((rows, kv), F32)]
    out += [jax.ShapeDtypeStruct((rows, kv), jnp.bfloat16)] * 3
    out += [jax.ShapeDtypeStruct((halo, kv), jnp.bfloat16)] * 2
    flops = 8 * SHARE * count * rows * HD * (keys - halo)
    return pl.pallas_call(
        functools.partial(part_kernel, heads, rows, halo),
        grid=(1,),
        out_shape=out,
        in_specs=[pl.BlockSpec(memory_space=pltpu.SMEM), q_spec, q_spec, h_spec, h_spec]
        + [whole_block(piece.shape) for piece in pieces]
        + [whole_block(after.shape)] * (GROUP + 1),
        out_specs=[whole_block(o.shape) for o in out],
        scratch_shapes=[
            pltpu.VMEM((keys, HD), jnp.bfloat16),
            pltpu.VMEM((keys, HD), jnp.bfloat16),
            pltpu.VMEM((halo + GROUP * rows, rows), F32),
            pltpu.VMEM((keys, HD), F32),
            pltpu.VMEM((keys, HD), F32),
        ],
        compiler_params=pltpu.CompilerParams(vmem_limit_bytes=24 * 2**20),
        cost_estimate=pl.CostEstimate(flops=flops, bytes_accessed=2**20, transcendentals=0),
    )(lengths, queries, grad_out, next_q, next_g, *pieces, *before, after)


def sum_kernel(parts, halo, *refs):
    out_ref = refs[-1]
    at = 0
    rows = out_ref.shape[1]
    terms = len(parts) * 4
    ends = refs[terms:-1]
    for which, heads in enumerate(parts):
        own, one, two, three = refs[at : at + 4]
        at += 4
        count = len(heads)
        for half in range(2):
            for i, head in enumerate(heads):
                cols = pl.ds((half * count + i) * HD, HD)
                total = own[:, cols] + one[:, cols].astype(F32) + two[:, cols].astype(F32) + three[:, cols].astype(F32)
                low, high = total[:halo], total[rows - halo :]
                for ref in ends[: GROUP * len(parts)][which :: len(parts)]:
                    high = high + ref[:, cols].astype(F32)
                low = low + ends[GROUP * len(parts) + which][:, cols].astype(F32)
                total = jnp.concatenate([low, total[halo : rows - halo], high], axis=0)
                out_ref[0, :, pl.ds((half * KVH + head) * HD, HD)] = total.astype(out_ref.dtype)


def on_device(queries, stash, grad_out, lengths):
    rows = queries.shape[1]
    pipe, ctx = lax.axis_size("pipe"), lax.axis_size("ctx")
    halo = -(-lengths.shape[0] // 16) * 16
    high = 1 << (pipe.bit_length() - 2)
    both = ("pipe", "ctx")

    def partner(block, step):
        route = [
            ((p ^ high) * ctx + c, p * ctx + d)
            for p in range(pipe)
            for c in range(ctx)
            for d in [step(c)]
            if d is not None and 0 <= d < ctx
        ]
        return lax.ppermute(block, both, route)

    def along(block, pick):
        return lax.ppermute(block, "ctx", [(c, d) for c in range(ctx) for d in [pick(c)] if d is not None and 0 <= d < ctx])

    kv = stash[0]
    before = partner(kv[rows - halo :], lambda c: c + 1 if c % GROUP == GROUP - 1 else None)
    after = partner(kv[:halo], lambda c: c - GROUP if c % GROUP == 0 else None)
    next_q = along(queries[0, :halo], lambda c: c - GROUP if c % GROUP == 0 else None)
    next_g = along(grad_out[0, :halo], lambda c: c - GROUP if c % GROUP == 0 else None)
    held = []
    for heads in PARTS:
        first, count = heads[0], len(heads)
        block = jnp.concatenate(
            [kv[:, first * HD : (first + count) * HD], kv[:, (KVH + first) * HD : (KVH + first + count) * HD]], axis=1
        )
        held.append(partner(block, lambda c: c))
    before = [before] + [along(before, lambda c: c + step if c % GROUP == 0 else None) for step in range(1, GROUP)]
    terms, ends_before, ends_after = [], [], []
    for heads, own in zip(PARTS, held):
        pieces = [own] + [along(own, lambda c: c ^ step) for step in range(1, GROUP)]
        mine, *others, to_before, to_after = part_grads(
            heads, halo, lengths, queries, grad_out, next_q, next_g, pieces, before, after
        )
        terms += [mine] + [along(other, lambda c: c ^ step) for step, other in zip(range(1, GROUP), others)]
        ends_before.append(to_before)
        ends_after.append(to_after)
    width = [end.shape[1] for end in ends_before]
    all_before = jnp.concatenate(ends_before, axis=1)
    all_after = jnp.concatenate(ends_after, axis=1)
    ends = []
    for rank in range(GROUP):
        got = along(all_before, lambda c: c - rank - 1 if c % GROUP == rank else None)
        ends += jnp.split(got, [sum(width[: i + 1]) for i in range(len(width) - 1)], axis=1)
    got = along(all_after, lambda c: c + GROUP if c % GROUP == 0 else None)
    ends += jnp.split(got, [sum(width[: i + 1]) for i in range(len(width) - 1)], axis=1)
    return pl.pallas_call(
        functools.partial(sum_kernel, PARTS, halo),
        out_shape=jax.ShapeDtypeStruct((1, rows, kv.shape[1]), jnp.bfloat16),
        compiler_params=pltpu.CompilerParams(vmem_limit_bytes=16 * 2**20),
    )(*terms, *ends)


def solution(mesh):
    placed = (P("pipe", "ctx", None), P("pipe", "ctx", None), P("pipe", "ctx", None), P())
    return jax.shard_map(
        on_device, mesh=mesh, in_specs=placed, out_specs=P("pipe", "ctx", None), check_vma=False
    )
```

```python
import functools
import math

import jax
import jax.numpy as jnp
from jax import lax
from jax.experimental import pallas as pl
from jax.experimental.pallas import tpu as pltpu
from jax.sharding import PartitionSpec as P

H = 32
KVH = 4
HD = 128
REACH = 5
GROUP = REACH - 1
SHARE = H // KVH
PARTS = KVH // 2
WIDE = SHARE * HD
MASKED = -1e30
F32 = jnp.float32
BF16 = jnp.bfloat16
NT = (((1,), (1,)), ((), ()))
NN = (((1,), (0,)), ((), ()))


def place():
    me = lax.axis_index("ctx")
    rank = lax.rem(me, GROUP)
    return me, rank, lax.rem(rank, 2)


def call(body, out, mib=8, flops=1000, **more):
    return pl.pallas_call(
        body,
        out_shape=out,
        compiler_params=pltpu.CompilerParams(vmem_limit_bytes=mib * 2**20),
        cost_estimate=pl.CostEstimate(flops=flops, bytes_accessed=1000, transcendentals=0),
        **more,
    )


def columns(head):
    return pl.ds(pl.multiple_of(head * HD, HD), HD)


def split_kernel(kv_ref, own, far):
    _, _, core = place()
    for part in range(PARTS):
        for half, ref in ((core, own), (1 - core, far)):
            for kind in range(2):
                ref[:, pl.ds((part * 2 + kind) * HD, HD)] = kv_ref[0, :, columns(half * PARTS + part + kind * KVH)]


def edge_rows(docs):
    return -(-SHARE * docs // 16) * 16


def hand_kernel(halo, docs, q_ref, g_ref, far, edge0, edge1, q_top, g_top, sem):
    _, _, core = place()
    rows = q_ref.shape[1]
    wide = PARTS * WIDE
    start = pl.multiple_of((1 - core) * wide, wide)
    tops = [(ref.at[0, pl.ds(0, halo)], top) for ref, top in ((q_ref, q_top), (g_ref, g_top))]
    whole = [
        (ref.at[0, :, pl.ds(start, wide)], far.at[pl.ds(at * rows, rows)]) for at, ref in enumerate((q_ref, g_ref))
    ]
    copies = [pltpu.make_async_copy(*copy, sem.at[at]) for at, copy in enumerate(tops + whole)]
    for copy in copies:
        copy.start()
    size = edge_rows(docs)
    to = lax.broadcasted_iota(jnp.int32, (size, SHARE * halo), 0)
    at = lax.broadcasted_iota(jnp.int32, (size, SHARE * halo), 1)
    picked = ((at // halo == to // docs) & (at % halo == to % docs)).astype(BF16)
    for copy in copies[:2]:
        copy.wait()
    for kind, top in enumerate((q_top, g_top)):
        for half, edge in enumerate((edge0, edge1)):
            for part in range(PARTS):
                heads = [(half * PARTS + part) * SHARE + head for head in range(SHARE)]
                block = jnp.concatenate([top[:, pl.ds(head * HD, HD)] for head in heads], axis=0)
                chosen = lax.dot_general(picked, block, NN, preferred_element_type=F32).astype(BF16)
                edge[pl.ds((kind * PARTS + part) * size, size), :] = chosen
    for copy in copies[2:]:
        copy.wait()


def edge_kernel(own, one, edge):
    _, rank, _ = place()
    halo = edge.shape[0]
    first = pl.ds(pl.multiple_of(jnp.where(rank < 2, 0, own.shape[0] - halo), 16), halo)
    edge[...] = jnp.where((rank == 0) | (rank == GROUP - 1), own[first, :], one[first, :])


def stage_kernel(q_ref, g_ref, far, edge0, edge1, q_buf, g_buf, sem):
    _, _, core = place()
    rows = q_ref.shape[1]
    copies = []
    for kind, (ref, buf) in enumerate(((q_ref, q_buf), (g_ref, g_buf))):
        for part in range(PARTS):
            for head in range(SHARE):
                here = head * rows
                mine = ref.at[0, :, columns((core * PARTS + part) * SHARE + head)]
                other = far.at[pl.ds(kind * rows, rows), pl.ds((part * SHARE + head) * HD, HD)]
                for slot, block in ((core, mine), (1 - core, other)):
                    at = pl.ds(pl.multiple_of(slot * WIDE + here, 16), rows)
                    copies.append((block, buf.at[part, at]))
    copies = [pltpu.make_async_copy(*copy, sem.at[at]) for at, copy in enumerate(copies)]
    for copy in copies:
        copy.start()
    size = edge0.shape[0] // (2 * PARTS)
    for half, edge in enumerate((edge0, edge1)):

        @pl.when(core == half)
        def _():
            extra = []
            for kind, buf in enumerate((q_buf, g_buf)):
                for part in range(PARTS):
                    block = edge.at[pl.ds((kind * PARTS + part) * size, size)]
                    to = buf.at[part, pl.ds(2 * WIDE, size)]
                    extra.append(pltpu.make_async_copy(block, to, sem.at[len(copies) + len(extra)]))
            for copy in extra:
                copy.start()
            for copy in extra:
                copy.wait()

    for copy in copies:
        copy.wait()


def doc_start(pos, len_ref):
    start = jnp.zeros_like(pos)
    end = jnp.int32(0)
    for doc in range(len_ref.shape[0]):
        end = end + len_ref[doc]
        start = jnp.where(end <= pos, end, start)
    return start


def bias_of(first_key, keys, query_pos, start):
    key_pos = first_key + lax.broadcasted_iota(jnp.int32, (keys, query_pos.shape[1]), 0)
    return jnp.where((key_pos >= start) & (key_pos <= query_pos), 0.0, MASKED)


def weigh(key, value, query, cot, bias, keep):
    scores = lax.dot_general(key, query, NT, preferred_element_type=F32) + bias
    top = jnp.max(scores, axis=0, keepdims=True)
    raw = jnp.exp2((scores - top) * (HD**-0.5 * math.log2(math.e)))
    weights = raw * (keep / jnp.sum(raw, axis=0, keepdims=True))
    dweights = lax.dot_general(value, cot, NT, preferred_element_type=F32)
    delta = jnp.sum(weights * dweights, axis=0, keepdims=True)
    dscores = weights * (dweights - delta)
    return weights.astype(BF16), dscores.astype(BF16)


def grad_kernel(halo, len_ref, q_buf, g_buf, own_ref, one_ref, two_ref, three_ref, edge_a, edge_b,
                own_out, one_out, two_out, three_out, end_a, end_b, k_buf, v_buf, dk_ref, dv_ref):
    rows = own_ref.shape[0]
    span = GROUP * rows
    me, rank, _ = place()
    first = (me - rank) * rows
    docs = len_ref.shape[0]
    scale = HD**-0.5

    for part in range(PARTS):
        here = part * 2 * HD
        k_cols, v_cols = pl.ds(here, HD), pl.ds(here + HD, HD)
        for buf, cols in ((k_buf, k_cols), (v_buf, v_cols)):
            for step, ref in enumerate((own_ref, one_ref, two_ref, three_ref)):
                buf[pl.ds(pl.multiple_of(halo + (rank ^ step) * rows, 16), rows), :] = ref[:, cols]
            buf[:halo, :] = jnp.where(rank < 2, edge_a[:, cols], edge_b[:, cols])
            buf[halo + span :, :] = edge_a[:, cols]
        dk_ref[...] = jnp.zeros_like(dk_ref)
        dv_ref[...] = jnp.zeros_like(dv_ref)

        for chip in range(2):

            @pl.when(rank // 2 == chip)
            def _():
                for slot in range(2):
                    block = 2 * chip + slot
                    keys = halo + (block + 1) * rows
                    cols = pl.ds(slot * WIDE, WIDE)
                    query_pos = first + block * rows + lax.broadcasted_iota(jnp.int32, (1, rows), 1)
                    start = doc_start(query_pos, len_ref)
                    keep = [jnp.where(start < first - halo, 0.0, 1.0)] * SHARE
                    if block == GROUP - 1:
                        keys = keys + halo
                        size = edge_rows(docs)
                        cols = pl.ds(slot * WIDE, WIDE + size)
                        lane = lax.broadcasted_iota(jnp.int32, (1, size), 1)
                        next_pos = first + span + lax.rem(lane, docs)
                        next_start = doc_start(next_pos, len_ref)
                        keep.append(jnp.where((next_start < first + span - halo) & (lane < SHARE * docs), 1.0, 0.0))
                    bias = [bias_of(first - halo, keys, query_pos, start)] * SHARE
                    if block == GROUP - 1:
                        bias.append(bias_of(first - halo, keys, next_pos, next_start))
                    query, cot = q_buf[part, cols, :], g_buf[part, cols, :]
                    weights, dscores = weigh(
                        k_buf[:keys, :], v_buf[:keys, :], query, cot,
                        jnp.concatenate(bias, axis=1), jnp.concatenate(keep, axis=1),
                    )
                    dv_ref[:keys, :] += lax.dot_general(weights, cot, NN, preferred_element_type=F32)
                    dk_ref[:keys, :] += lax.dot_general(dscores, query, NN, preferred_element_type=F32)

        def terms(row, size):
            at = pl.ds(pl.multiple_of(row, 16), size)
            return ((k_cols, dk_ref[at, :] * scale), (v_cols, dv_ref[at, :]))

        for step, ref in enumerate((own_out, one_out)):
            for cols, term in terms(halo + (rank ^ step) * rows, rows):
                ref[:, cols] = term.astype(ref.dtype)
        for step, ref in ((2, two_out), (3, three_out)):
            for cols, term in terms(jnp.where(rank < 2, 0, halo + (rank ^ step) * rows), rows):
                ref[:, cols] = term.astype(ref.dtype)
        for ref, giver in ((end_a, 2), (end_b, 3)):
            for cols, term in terms(jnp.where(rank == giver, halo + span, 0), halo):
                ref[:, cols] = term.astype(ref.dtype)


def grads(halo, *inputs):
    rows = inputs[3].shape[0]
    wide = 2 * PARTS * HD
    total = (halo + GROUP * rows + halo, HD)
    out = [jax.ShapeDtypeStruct((rows, wide), F32)]
    out += [jax.ShapeDtypeStruct((rows, wide), BF16)] * 3
    out += [jax.ShapeDtypeStruct((halo, wide), BF16)] * 2
    vmem = pl.BlockSpec(memory_space=pltpu.VMEM)
    return call(
        functools.partial(grad_kernel, halo),
        out,
        in_specs=[pl.BlockSpec(memory_space=pltpu.SMEM)] + [vmem] * (len(inputs) - 1),
        scratch_shapes=[
            pltpu.VMEM(total, BF16),
            pltpu.VMEM(total, BF16),
            pltpu.VMEM(total, F32),
            pltpu.VMEM(total, F32),
        ],
        mib=24,
        flops=COST,
    )(*inputs)


COST = 4 * 10**9


def sum_kernel(halo, own, one, two, three, end_a, end_b, out_ref):
    _, rank, core = place()
    rows = out_ref.shape[1]
    chip0, last = rank < 2, rank == GROUP - 1
    for part in range(PARTS):
        for kind in range(2):
            cols = pl.ds((part * 2 + kind) * HD, HD)
            ones, twos, threes, a, b = (ref[:, cols].astype(F32) for ref in (one, two, three, end_a, end_b))
            mine = own[:, cols] + jnp.where(chip0, twos, 0.0)
            other = ones + jnp.where(chip0, threes, 0.0)
            highs = (threes[:halo] + b, twos[:halo] + a)
            lows = (a, b)
            for half in range(2):
                total = jnp.where(core == half, mine, other)
                high = jnp.where(last, highs[half], 0.0)
                low = jnp.where(rank == 0, lows[half], 0.0)
                total = jnp.concatenate(
                    [total[:halo] + low, total[halo : rows - halo], total[rows - halo :] + high], axis=0
                )
                out_ref[0, :, pl.ds((kind * KVH + half * PARTS + part) * HD, HD)] = total.astype(out_ref.dtype)


def on_device(queries, stash, grad_out, lengths):
    rows = queries.shape[1]
    pipe, ctx = lax.axis_size("pipe"), lax.axis_size("ctx")
    halo = -(-lengths.shape[0] // 16) * 16
    high = 1 << (pipe.bit_length() - 2)

    def pairs(pick):
        return [(c, (c + pick[c % GROUP]) % ctx) for c in range(ctx)]

    def partner(block, pick):
        route = [((p ^ high) * ctx + c, p * ctx + d) for p in range(pipe) for c, d in pairs(pick)]
        return lax.ppermute(block, ("pipe", "ctx"), route)

    def along(block, pick):
        return lax.ppermute(block, "ctx", pairs(pick))

    stay = (0,) * GROUP
    flip = [tuple((rank ^ step) - rank for rank in range(GROUP)) for step in range(GROUP)]

    def shape(*dims):
        return jax.ShapeDtypeStruct(dims, BF16)

    def after(value, *others):
        return lax.optimization_barrier((value, *others))[0]

    edge_wide = 2 * PARTS * HD
    hbm = pl.BlockSpec(memory_space=pltpu.HBM)
    held = partner(stash, stay)

    wide = PARTS * WIDE
    size = edge_rows(lengths.shape[0])

    def beside(queries, grad_out):
        far, edge0, edge1 = call(
            functools.partial(hand_kernel, halo, lengths.shape[0]),
            [shape(2 * rows, wide), *[shape(2 * PARTS * size, HD)] * 2],
            in_specs=[hbm] * 2,
            scratch_shapes=[pltpu.VMEM((halo, 2 * wide), BF16)] * 2 + [pltpu.SemaphoreType.DMA((4,))],
        )(queries, grad_out)
        return along(far, flip[1]), along(edge0, (-2, -2, 2, 2)), along(edge1, (-1, -3, 3, 1))

    def nothing(*_):
        return jnp.zeros((2 * rows, wide), BF16), *[jnp.zeros((2 * PARTS * size, HD), BF16)] * 2

    far, edge0, edge1 = lax.cond(lengths[0] > 0, beside, nothing, queries, grad_out)
    q_buf, g_buf = call(
        stage_kernel,
        [shape(PARTS, 2 * WIDE + size, HD)] * 2,
        in_specs=[hbm] * 5,
        scratch_shapes=[pltpu.SemaphoreType.DMA((4 * PARTS * SHARE + 2 * PARTS,))],
    )(queries, grad_out, far, edge0, edge1)
    held, q_buf, g_buf = lax.optimization_barrier((held, q_buf, g_buf))
    own, far = call(split_kernel, [shape(rows, edge_wide)] * 2)(held)

    got = [own, along(far, flip[1]), along(own, flip[2]), along(far, flip[3])]
    edge = call(edge_kernel, shape(halo, edge_wide))(own, got[1])
    edge_a, edge_b = along(edge, (-2, -2, 2, 2)), along(edge, (4, 4, 4, 4))
    own, one, two, three, end_a, end_b = grads(halo, lengths, q_buf, g_buf, *got, edge_a, edge_b)
    back = (
        along(one, flip[1]),
        along(two, (-2, -2, -2, -2)),
        along(three, (-1, -3, -1, -3)),
        along(end_a, (-2, 4, 2, -4)),
        along(end_b, (-2, 4, -3, 1)),
    )
    return call(functools.partial(sum_kernel, halo), shape(1, rows, 2 * KVH * HD))(own, *back)


def solution(mesh):
    placed = (P("pipe", "ctx", None), P("pipe", "ctx", None), P("pipe", "ctx", None), P())
    return jax.shard_map(
        on_device, mesh=mesh, in_specs=placed, out_specs=P("pipe", "ctx", None), check_vma=False
    )
```

```python
import functools
import math

import jax
import jax.numpy as jnp
from jax import lax
from jax.experimental import pallas as pl
from jax.experimental.pallas import tpu as pltpu
from jax.sharding import PartitionSpec as P

H = 32
KVH = 4
HD = 128
REACH = 5
GROUP = REACH - 1
SHARE = H // KVH
PARTS = KVH // 2
WIDE = SHARE * HD
MASKED = -1e30
F32 = jnp.float32
BF16 = jnp.bfloat16
NT = (((1,), (1,)), ((), ()))
NN = (((1,), (0,)), ((), ()))


def place():
    me = lax.axis_index("ctx")
    rank = lax.rem(me, GROUP)
    return me, rank, lax.rem(rank, 2)


def call(body, out, mib=8, flops=1000, **more):
    return pl.pallas_call(
        body,
        out_shape=out,
        compiler_params=pltpu.CompilerParams(vmem_limit_bytes=mib * 2**20),
        cost_estimate=pl.CostEstimate(flops=flops, bytes_accessed=1000, transcendentals=0),
        **more,
    )


def columns(head):
    return pl.ds(pl.multiple_of(head * HD, HD), HD)


def split_kernel(kv_ref, far, *parts):
    _, _, core = place()
    for half, refs in ((core, parts[:PARTS]), (1 - core, parts[PARTS:])):
        for part, ref in enumerate(refs):
            for kind in range(2):
                block = kv_ref[0, :, columns(half * PARTS + part + kind * KVH)]
                ref[:, pl.ds(kind * HD, HD)] = block
                if half is not core:
                    far[:, pl.ds((part * 2 + kind) * HD, HD)] = block


def edge_rows(docs):
    return -(-SHARE * docs // 16) * 16


def hand_kernel(halo, docs, q_ref, g_ref, far, edge0, edge1, q_top, g_top, sem):
    _, _, core = place()
    rows = q_ref.shape[1]
    wide = PARTS * WIDE
    start = pl.multiple_of((1 - core) * wide, wide)
    tops = [(ref.at[0, pl.ds(0, halo)], top) for ref, top in ((q_ref, q_top), (g_ref, g_top))]
    whole = [
        (ref.at[0, :, pl.ds(start, wide)], far.at[pl.ds(at * rows, rows)]) for at, ref in enumerate((q_ref, g_ref))
    ]
    copies = [pltpu.make_async_copy(*copy, sem.at[at]) for at, copy in enumerate(tops + whole)]
    for copy in copies:
        copy.start()
    size = edge_rows(docs)
    to = lax.broadcasted_iota(jnp.int32, (size, SHARE * halo), 0)
    at = lax.broadcasted_iota(jnp.int32, (size, SHARE * halo), 1)
    picked = ((at // halo == to // docs) & (at % halo == to % docs)).astype(BF16)
    for copy in copies[:2]:
        copy.wait()
    for kind, top in enumerate((q_top, g_top)):
        for half, edge in enumerate((edge0, edge1)):
            for part in range(PARTS):
                heads = [(half * PARTS + part) * SHARE + head for head in range(SHARE)]
                block = jnp.concatenate([top[:, pl.ds(head * HD, HD)] for head in heads], axis=0)
                chosen = lax.dot_general(picked, block, NN, preferred_element_type=F32).astype(BF16)
                edge[pl.ds((kind * PARTS + part) * size, size), :] = chosen
    for copy in copies[2:]:
        copy.wait()


def edge_kernel(*refs):
    *own, one, edge = refs
    _, rank, _ = place()
    halo = edge.shape[0]
    first = pl.ds(pl.multiple_of(jnp.where(rank < 2, 0, one.shape[0] - halo), 16), halo)
    for part, ref in enumerate(own):
        cols = pl.ds(part * 2 * HD, 2 * HD)
        edge[:, cols] = jnp.where((rank == 0) | (rank == GROUP - 1), ref[first, :], one[first, cols])


def stage_kernel(q_ref, g_ref, far, edge0, edge1, q_buf, g_buf, sem):
    _, _, core = place()
    rows = q_ref.shape[1]
    copies = []
    for kind, (ref, buf) in enumerate(((q_ref, q_buf), (g_ref, g_buf))):
        for part in range(PARTS):
            for head in range(SHARE):
                here = head * rows
                mine = ref.at[0, :, columns((core * PARTS + part) * SHARE + head)]
                other = far.at[pl.ds(kind * rows, rows), pl.ds((part * SHARE + head) * HD, HD)]
                for slot, block in ((core, mine), (1 - core, other)):
                    at = pl.ds(pl.multiple_of(slot * WIDE + here, 16), rows)
                    copies.append((block, buf.at[part, at]))
    copies = [pltpu.make_async_copy(*copy, sem.at[at]) for at, copy in enumerate(copies)]
    for copy in copies:
        copy.start()
    size = edge0.shape[0] // (2 * PARTS)
    for half, edge in enumerate((edge0, edge1)):

        @pl.when(core == half)
        def _():
            extra = []
            for kind, buf in enumerate((q_buf, g_buf)):
                for part in range(PARTS):
                    block = edge.at[pl.ds((kind * PARTS + part) * size, size)]
                    to = buf.at[part, pl.ds(2 * WIDE, size)]
                    extra.append(pltpu.make_async_copy(block, to, sem.at[len(copies) + len(extra)]))
            for copy in extra:
                copy.start()
            for copy in extra:
                copy.wait()

    for copy in copies:
        copy.wait()


def doc_start(pos, len_ref):
    start = jnp.zeros_like(pos)
    end = jnp.int32(0)
    for doc in range(len_ref.shape[0]):
        end = end + len_ref[doc]
        start = jnp.where(end <= pos, end, start)
    return start


def bias_of(first_key, keys, query_pos, start):
    key_pos = first_key + lax.broadcasted_iota(jnp.int32, (keys, query_pos.shape[1]), 0)
    return jnp.where((key_pos >= start) & (key_pos <= query_pos), 0.0, MASKED)


def weigh(key, value, query, cot, bias, keep):
    scores = lax.dot_general(key, query, NT, preferred_element_type=F32) + bias
    top = jnp.max(scores, axis=0, keepdims=True)
    raw = jnp.exp2((scores - top) * (HD**-0.5 * math.log2(math.e)))
    dweights = lax.dot_general(value, cot, NT, preferred_element_type=F32)
    share = keep / jnp.sum(raw, axis=0, keepdims=True)
    delta = jnp.sum(raw * dweights, axis=0, keepdims=True) * share
    weights = raw * share
    dscores = weights * (dweights - delta)
    return weights.astype(BF16), dscores.astype(BF16)


def grad_kernel(stage, halo, len_ref, q_buf, g_buf, *refs):
    if stage:
        dk_last, dv_last, *refs = refs
    *got, edge_a, edge_b, dk_ref, dv_ref, k_buf, v_buf = refs
    rows = got[0].shape[0]
    span = GROUP * rows
    me, rank, _ = place()
    first = (me - rank) * rows
    docs = len_ref.shape[0]

    def load(part, blocks):
        here = pl.ds(part * 2 * HD, 2 * HD)
        low, high = jnp.where(rank < 2, edge_a[:, here], edge_b[:, here]), edge_b[:, here]
        for buf, kind in ((k_buf, 0), (v_buf, HD)):
            for step, block in enumerate(blocks):
                at = pl.ds(pl.multiple_of(halo + (rank ^ step) * rows, 16), rows)
                buf[part, at, :] = block[:, kind : kind + HD]
            buf[part, :halo, :] = low[:, kind : kind + HD]
            buf[part, halo + span :, :] = high[:, kind : kind + HD]

    own, one, two, three = got[:4]
    here = pl.ds(stage * 2 * HD, 2 * HD)
    load(stage, (own[...], one[:, here], two[...], three[...]))
    if stage:
        dk_ref[...] = dk_last[...]
        dv_ref[...] = dv_last[...]
    else:
        for part, own in enumerate(got[4:], 1):
            load(part, (own[...], one[:, pl.ds(part * 2 * HD, 2 * HD)]))
        dk_ref[...] = jnp.zeros_like(dk_ref)
        dv_ref[...] = jnp.zeros_like(dv_ref)

    for chip in range(2):

        @pl.when(rank // 2 == chip)
        def _():
            tiles = []
            for part in (stage,) if chip else range(0 if stage == 0 else PARTS, PARTS):
                for slot in range(2):
                    block = 2 * chip + slot
                    query_pos = first + block * rows + lax.broadcasted_iota(jnp.int32, (1, rows), 1)
                    start = doc_start(query_pos, len_ref)
                    keep = jnp.where(start < first - halo, 0.0, 1.0)
                    tiles.append((part, pl.ds(slot * WIDE, WIDE), 0, halo + (block + 1) * rows, query_pos, start, keep, SHARE))
            if chip == 0:
                size = edge_rows(docs)
                lane = lax.broadcasted_iota(jnp.int32, (1, size), 1)
                query_pos = first + span + lax.rem(lane, docs)
                start = doc_start(query_pos, len_ref)
                keep = jnp.where((start < first + span - halo) & (lane < SHARE * docs), 1.0, 0.0)
                tiles.append((stage, pl.ds(2 * WIDE, size), halo, halo + span + halo, query_pos, start, keep, 1))
            for part, cols, low, high, query_pos, start, keep, times in tiles:
                keys = pl.ds(low, high - low)
                bias = bias_of(first - halo + low, high - low, query_pos, start)
                query, cot = q_buf[part, cols, :], g_buf[part, cols, :]
                weights, dscores = weigh(
                    k_buf[part, keys, :], v_buf[part, keys, :], query, cot,
                    jnp.concatenate([bias] * times, axis=1), jnp.concatenate([keep] * times, axis=1),
                )
                dv_ref[part, keys, :] += lax.dot_general(weights, cot, NN, preferred_element_type=F32)
                dk_ref[part, keys, :] += lax.dot_general(dscores, query, NN, preferred_element_type=F32)


def terms(dk_ref, dv_ref, part, row, size):
    at = pl.ds(row if isinstance(row, int) else pl.multiple_of(row, 16), size)
    return jnp.concatenate([dk_ref[part, at, :] * HD**-0.5, dv_ref[part, at, :]], axis=1)


def across_kernel(part, halo, dk_ref, dv_ref, across):
    _, rank, _ = place()
    kv = 2 * HD
    rows = across.shape[0] - (0 if part else halo)
    for which in range(PARTS):
        cols = pl.ds(which * kv, kv)
        across[:rows, cols] = terms(dk_ref, dv_ref, part, halo + (rank ^ (2 + which)) * rows, rows).astype(BF16)
        if not part:
            across[rows:, cols] = terms(dk_ref, dv_ref, which, 0, halo).astype(BF16)


def ends_kernel(halo, dk_ref, dv_ref, across, ends):
    _, rank, _ = place()
    kv = 2 * HD
    rows = across.shape[0] - halo
    for part in range(PARTS):
        cols = pl.ds(part * kv, kv)
        before = terms(dk_ref, dv_ref, part, 0, halo) + across[rows:, cols].astype(F32)
        behind = terms(dk_ref, dv_ref, part, halo + GROUP * rows, halo)
        ends[:, cols] = jnp.where(rank < 2, behind, before).astype(BF16)


def join_kernel(dk_ref, dv_ref, across0, across1, ends, mine, other):
    kv = 2 * HD
    halo, (rows, _) = ends.shape[0], mine.shape
    _, rank, _ = place()
    for ref, step, first, last in ((mine, 0, 0, GROUP - 1), (other, 1, 1, GROUP - 2)):
        for part, across in enumerate((across0, across1)):
            cols = pl.ds(part * kv, kv)
            total = terms(dk_ref, dv_ref, part, halo + (rank ^ step) * rows, rows)
            total = total + across[:rows, pl.ds(step * kv, kv)].astype(F32)
            end = ends[:, cols].astype(F32)
            low = total[:halo] + jnp.where(rank == first, end, 0.0)
            high = total[rows - halo :] + jnp.where(rank == last, end, 0.0)
            ref[:, cols] = jnp.concatenate([low, total[halo : rows - halo], high], axis=0).astype(ref.dtype)


def grads(stage, halo, rows, *inputs):
    total = (PARTS, halo + GROUP * rows + halo, HD)
    vmem = pl.BlockSpec(memory_space=pltpu.VMEM)
    return call(
        functools.partial(grad_kernel, stage, halo),
        [jax.ShapeDtypeStruct(total, F32)] * 2,
        in_specs=[pl.BlockSpec(memory_space=pltpu.SMEM)] + [vmem] * (len(inputs) - 1),
        scratch_shapes=[pltpu.VMEM(total, BF16)] * 2,
        mib=24,
        flops=COST,
    )(*inputs)


COST = 4 * 10**9


def place_kernel(mine, other, out_ref):
    _, _, core = place()
    for part in range(PARTS):
        for kind in range(2):
            cols = pl.ds((part * 2 + kind) * HD, HD)
            for half in range(2):
                total = jnp.where(core == half, mine[:, cols], other[:, cols].astype(F32))
                out_ref[0, :, pl.ds((kind * KVH + half * PARTS + part) * HD, HD)] = total.astype(out_ref.dtype)


def on_device(queries, stash, grad_out, lengths):
    rows = queries.shape[1]
    pipe, ctx = lax.axis_size("pipe"), lax.axis_size("ctx")
    halo = -(-lengths.shape[0] // 16) * 16
    high = 1 << (pipe.bit_length() - 2)

    def pairs(pick):
        return [(c, (c + pick[c % GROUP]) % ctx) for c in range(ctx)]

    def partner(block, pick):
        route = [((p ^ high) * ctx + c, p * ctx + d) for p in range(pipe) for c, d in pairs(pick)]
        return lax.ppermute(block, ("pipe", "ctx"), route)

    def along(block, pick):
        return lax.ppermute(block, "ctx", pairs(pick))

    stay = (0,) * GROUP
    flip = [tuple((rank ^ step) - rank for rank in range(GROUP)) for step in range(GROUP)]

    def shape(*dims):
        return jax.ShapeDtypeStruct(dims, BF16)

    def after(value, *others):
        return lax.optimization_barrier((value, *others))[0]

    edge_wide = 2 * PARTS * HD
    hbm = pl.BlockSpec(memory_space=pltpu.HBM)
    held = partner(stash, stay)

    wide = PARTS * WIDE
    size = edge_rows(lengths.shape[0])

    def beside(queries, grad_out):
        far, edge0, edge1 = call(
            functools.partial(hand_kernel, halo, lengths.shape[0]),
            [shape(2 * rows, wide), *[shape(2 * PARTS * size, HD)] * 2],
            in_specs=[hbm] * 2,
            scratch_shapes=[pltpu.VMEM((halo, 2 * wide), BF16)] * 2 + [pltpu.SemaphoreType.DMA((4,))],
        )(queries, grad_out)
        return along(far, flip[1]), along(edge0, (-4, -4, 4, 4)), along(edge1, (-3, -5, 5, 3))

    def nothing(*_):
        return jnp.zeros((2 * rows, wide), BF16), *[jnp.zeros((2 * PARTS * size, HD), BF16)] * 2

    far, edge0, edge1 = lax.cond(lengths[0] > 0, beside, nothing, queries, grad_out)
    q_buf, g_buf = call(
        stage_kernel,
        [shape(PARTS, 2 * WIDE + size, HD)] * 2,
        in_specs=[hbm] * 5,
        scratch_shapes=[pltpu.SemaphoreType.DMA((4 * PARTS * SHARE + 2 * PARTS,))],
    )(queries, grad_out, far, edge0, edge1)
    held, q_buf, g_buf = lax.optimization_barrier((held, q_buf, g_buf))
    far, *parts = call(split_kernel, [shape(rows, edge_wide), *[shape(rows, 2 * HD)] * (2 * PARTS)])(held)
    owns, fars = parts[:PARTS], parts[PARTS:]

    one = along(far, flip[1])
    got = [(own, one, along(own, flip[2]), along(far, flip[3])) for own, far in zip(owns, fars)]
    edge = call(edge_kernel, shape(halo, edge_wide))(*owns, one)
    edges = along(edge, (2, 2, 2, 2)), along(edge, (-4, -4, 4, 4))
    raw = grads(0, halo, rows, lengths, q_buf, g_buf, *got[0], *owns[1:], *edges)
    first = call(functools.partial(across_kernel, 0, halo), shape(rows + halo, edge_wide))(*raw)
    first = along(first, flip[2])
    raw = grads(1, halo, rows, lengths, q_buf, g_buf, *raw, *got[1], *edges)
    second = along(call(functools.partial(across_kernel, 1, halo), shape(rows, edge_wide))(*raw), flip[2])
    ends = along(call(functools.partial(ends_kernel, halo), shape(halo, edge_wide))(*raw, first), (4, 4, -4, -4))
    mine, other = call(
        join_kernel, [jax.ShapeDtypeStruct((rows, edge_wide), F32), shape(rows, edge_wide)]
    )(*raw, first, second, ends)
    return call(place_kernel, shape(1, rows, 2 * KVH * HD))(mine, along(other, flip[1]))


def solution(mesh):
    placed = (P("pipe", "ctx", None), P("pipe", "ctx", None), P("pipe", "ctx", None), P())
    return jax.shard_map(
        on_device, mesh=mesh, in_specs=placed, out_specs=P("pipe", "ctx", None), check_vma=False
    )
```

```python
import functools
import math

import jax
import jax.numpy as jnp
from jax import lax
from jax.experimental import pallas as pl
from jax.experimental.pallas import tpu as pltpu
from jax.sharding import PartitionSpec as P

H = 32
KVH = 4
HD = 128
REACH = 5
GROUP = REACH - 1
SHARE = H // KVH
PARTS = KVH // 2
WIDE = SHARE * HD
MASKED = -1e30
F32 = jnp.float32
BF16 = jnp.bfloat16
NT = (((1,), (1,)), ((), ()))
NN = (((1,), (0,)), ((), ()))


def place():
    me = lax.axis_index("ctx")
    rank = lax.rem(me, GROUP)
    return me, rank, lax.rem(rank, 2)


def call(body, out, mib=8, flops=1000, **more):
    return pl.pallas_call(
        body,
        out_shape=out,
        compiler_params=pltpu.CompilerParams(vmem_limit_bytes=mib * 2**20),
        cost_estimate=pl.CostEstimate(flops=flops, bytes_accessed=1000, transcendentals=0),
        **more,
    )


def columns(head):
    return pl.ds(pl.multiple_of(head * HD, HD), HD)


def split_kernel(kv_ref, far, *parts):
    _, _, core = place()
    for half, refs in ((core, parts[:PARTS]), (1 - core, parts[PARTS:])):
        for part, ref in enumerate(refs):
            for kind in range(2):
                block = kv_ref[0, :, columns(half * PARTS + part + kind * KVH)]
                ref[:, pl.ds(kind * HD, HD)] = block
                if half is not core:
                    far[:, pl.ds((part * 2 + kind) * HD, HD)] = block


def edge_rows(docs):
    return -(-SHARE * docs // 16) * 16


def hand_kernel(halo, docs, q_ref, g_ref, far, edge0, edge1, q_top, g_top, sem):
    _, _, core = place()
    rows = q_ref.shape[1]
    wide = PARTS * WIDE
    start = pl.multiple_of((1 - core) * wide, wide)
    tops = [(ref.at[0, pl.ds(0, halo)], top) for ref, top in ((q_ref, q_top), (g_ref, g_top))]
    whole = [
        (ref.at[0, :, pl.ds(start, wide)], far.at[pl.ds(at * rows, rows)]) for at, ref in enumerate((q_ref, g_ref))
    ]
    copies = [pltpu.make_async_copy(*copy, sem.at[at]) for at, copy in enumerate(tops + whole)]
    for copy in copies:
        copy.start()
    size = edge_rows(docs)
    to = lax.broadcasted_iota(jnp.int32, (size, SHARE * halo), 0)
    at = lax.broadcasted_iota(jnp.int32, (size, SHARE * halo), 1)
    picked = ((at // halo == to // docs) & (at % halo == to % docs)).astype(BF16)
    for copy in copies[:2]:
        copy.wait()
    for kind, top in enumerate((q_top, g_top)):
        for half, edge in enumerate((edge0, edge1)):
            for part in range(PARTS):
                heads = [(half * PARTS + part) * SHARE + head for head in range(SHARE)]
                block = jnp.concatenate([top[:, pl.ds(head * HD, HD)] for head in heads], axis=0)
                chosen = lax.dot_general(picked, block, NN, preferred_element_type=F32).astype(BF16)
                edge[pl.ds((kind * PARTS + part) * size, size), :] = chosen
    for copy in copies[2:]:
        copy.wait()


def edge_kernel(*refs):
    *own, one, edge = refs
    _, rank, _ = place()
    halo = edge.shape[0]
    first = pl.ds(pl.multiple_of(jnp.where(rank < 2, 0, one.shape[0] - halo), 16), halo)
    for part, ref in enumerate(own):
        cols = pl.ds(part * 2 * HD, 2 * HD)
        edge[:, cols] = jnp.where((rank == 0) | (rank == GROUP - 1), ref[first, :], one[first, cols])


def stage_kernel(q_ref, g_ref, far, edge0, edge1, q_buf, g_buf, sem):
    _, _, core = place()
    rows = q_ref.shape[1]
    copies = []
    for kind, (ref, buf) in enumerate(((q_ref, q_buf), (g_ref, g_buf))):
        for part in range(PARTS):
            for head in range(SHARE):
                here = head * rows
                mine = ref.at[0, :, columns((core * PARTS + part) * SHARE + head)]
                other = far.at[pl.ds(kind * rows, rows), pl.ds((part * SHARE + head) * HD, HD)]
                for slot, block in ((core, mine), (1 - core, other)):
                    at = pl.ds(pl.multiple_of(slot * WIDE + here, 16), rows)
                    copies.append((block, buf.at[part, at]))
    copies = [pltpu.make_async_copy(*copy, sem.at[at]) for at, copy in enumerate(copies)]
    for copy in copies:
        copy.start()
    size = edge0.shape[0] // (2 * PARTS)
    for half, edge in enumerate((edge0, edge1)):

        @pl.when(core == half)
        def _():
            extra = []
            for kind, buf in enumerate((q_buf, g_buf)):
                for part in range(PARTS):
                    block = edge.at[pl.ds((kind * PARTS + part) * size, size)]
                    to = buf.at[part, pl.ds(2 * WIDE, size)]
                    extra.append(pltpu.make_async_copy(block, to, sem.at[len(copies) + len(extra)]))
            for copy in extra:
                copy.start()
            for copy in extra:
                copy.wait()

    for copy in copies:
        copy.wait()


def doc_start(pos, len_ref):
    start = jnp.zeros_like(pos)
    end = jnp.int32(0)
    for doc in range(len_ref.shape[0]):
        end = end + len_ref[doc]
        start = jnp.where(end <= pos, end, start)
    return start


def bias_of(first_key, keys, query_pos, start):
    key_pos = first_key + lax.broadcasted_iota(jnp.int32, (keys, query_pos.shape[1]), 0)
    return jnp.where((key_pos >= start) & (key_pos <= query_pos), 0.0, MASKED)


def raise_scores(key, query, bias):
    return lax.dot_general(key, query, NT, preferred_element_type=F32) + bias


def softmax(scores, keep):
    top = jnp.max(scores, axis=0, keepdims=True)
    raw = jnp.exp2((scores - top) * (HD**-0.5 * math.log2(math.e)))
    return raw * (keep / jnp.sum(raw, axis=0, keepdims=True))


def grad_kernel(stage, halo, len_ref, q_buf, g_buf, *refs):
    if stage:
        dk_last, dv_last, *refs = refs
    *got, edge_a, edge_b, dk_ref, dv_ref, k_buf, v_buf = refs
    rows = got[0].shape[0]
    span = GROUP * rows
    me, rank, _ = place()
    first = (me - rank) * rows
    docs = len_ref.shape[0]

    def load(part, blocks):
        here = pl.ds(part * 2 * HD, 2 * HD)
        low, high = jnp.where(rank < 2, edge_a[:, here], edge_b[:, here]), edge_b[:, here]
        for buf, kind in ((k_buf, 0), (v_buf, HD)):
            for step, block in enumerate(blocks):
                at = pl.ds(pl.multiple_of(halo + (rank ^ step) * rows, 16), rows)
                buf[part, at, :] = block[:, kind : kind + HD]
            buf[part, :halo, :] = low[:, kind : kind + HD]
            buf[part, halo + span :, :] = high[:, kind : kind + HD]

    own, one, two, three = got[:4]
    here = pl.ds(stage * 2 * HD, 2 * HD)
    load(stage, (own[...], one[:, here], two[...], three[...]))
    if stage:
        dk_ref[...] = dk_last[...]
        dv_ref[...] = dv_last[...]
    else:
        for part, own in enumerate(got[4:], 1):
            load(part, (own[...], one[:, pl.ds(part * 2 * HD, 2 * HD)]))
        dk_ref[...] = jnp.zeros_like(dk_ref)
        dv_ref[...] = jnp.zeros_like(dv_ref)

    for chip in range(2):

        @pl.when(rank // 2 == chip)
        def _():
            tiles = []
            for part in (stage,) if chip else range(0 if stage == 0 else PARTS, PARTS):
                for slot in range(2):
                    block = 2 * chip + slot
                    query_pos = first + block * rows + lax.broadcasted_iota(jnp.int32, (1, rows), 1)
                    start = doc_start(query_pos, len_ref)
                    keep = jnp.where(start < first - halo, 0.0, 1.0)
                    tiles.append((part, pl.ds(slot * WIDE, WIDE), 0, halo + (block + 1) * rows, query_pos, start, keep, SHARE))
            if chip == 0:
                size = edge_rows(docs)
                lane = lax.broadcasted_iota(jnp.int32, (1, size), 1)
                query_pos = first + span + lax.rem(lane, docs)
                start = doc_start(query_pos, len_ref)
                keep = jnp.where((start < first + span - halo) & (lane < SHARE * docs), 1.0, 0.0)
                tiles.append((stage, pl.ds(2 * WIDE, size), halo, halo + span + halo, query_pos, start, keep, 1))
            def raised(tile):
                part, cols, low, high, query_pos, start, keep, times = tile
                bias = bias_of(first - halo + low, high - low, query_pos, start)
                bias = jnp.concatenate([bias] * times, axis=1)
                return raise_scores(k_buf[part, pl.ds(low, high - low), :], q_buf[part, cols, :], bias)

            scores = raised(tiles[0])
            for at, (part, cols, low, high, query_pos, start, keep, times) in enumerate(tiles):
                keys = pl.ds(low, high - low)
                query, cot = q_buf[part, cols, :], g_buf[part, cols, :]
                weights = softmax(scores, jnp.concatenate([keep] * times, axis=1))
                dweights = lax.dot_general(v_buf[part, keys, :], cot, NT, preferred_element_type=F32)
                dv_ref[part, keys, :] += lax.dot_general(weights.astype(BF16), cot, NN, preferred_element_type=F32)
                if at + 1 < len(tiles):
                    scores = raised(tiles[at + 1])
                delta = jnp.sum(weights * dweights, axis=0, keepdims=True)
                dscores = (weights * (dweights - delta)).astype(BF16)
                dk_ref[part, keys, :] += lax.dot_general(dscores, query, NN, preferred_element_type=F32)


def terms(dk_ref, dv_ref, part, row, size):
    at = pl.ds(row if isinstance(row, int) else pl.multiple_of(row, 16), size)
    return jnp.concatenate([dk_ref[part, at, :] * HD**-0.5, dv_ref[part, at, :]], axis=1)


def across_kernel(part, halo, dk_ref, dv_ref, across):
    _, rank, _ = place()
    kv = 2 * HD
    rows = across.shape[0] - (0 if part else halo)
    for which in range(PARTS):
        cols = pl.ds(which * kv, kv)
        across[:rows, cols] = terms(dk_ref, dv_ref, part, halo + (rank ^ (2 + which)) * rows, rows).astype(BF16)
        if not part:
            across[rows:, cols] = terms(dk_ref, dv_ref, which, 0, halo).astype(BF16)


def ends_kernel(halo, dk_ref, dv_ref, across, ends):
    _, rank, _ = place()
    kv = 2 * HD
    rows = across.shape[0] - halo
    for part in range(PARTS):
        cols = pl.ds(part * kv, kv)
        before = terms(dk_ref, dv_ref, part, 0, halo) + across[rows:, cols].astype(F32)
        behind = terms(dk_ref, dv_ref, part, halo + GROUP * rows, halo)
        ends[:, cols] = jnp.where(rank < 2, behind, before).astype(BF16)


def join_kernel(dk_ref, dv_ref, across0, across1, ends, mine, other):
    kv = 2 * HD
    halo, (rows, _) = ends.shape[0], mine.shape
    _, rank, _ = place()
    for ref, step, first, last in ((mine, 0, 0, GROUP - 1), (other, 1, 1, GROUP - 2)):
        for part, across in enumerate((across0, across1)):
            cols = pl.ds(part * kv, kv)
            total = terms(dk_ref, dv_ref, part, halo + (rank ^ step) * rows, rows)
            total = total + across[:rows, pl.ds(step * kv, kv)].astype(F32)
            end = ends[:, cols].astype(F32)
            low = total[:halo] + jnp.where(rank == first, end, 0.0)
            high = total[rows - halo :] + jnp.where(rank == last, end, 0.0)
            ref[:, cols] = jnp.concatenate([low, total[halo : rows - halo], high], axis=0).astype(ref.dtype)


def grads(stage, halo, rows, *inputs):
    total = (PARTS, halo + GROUP * rows + halo, HD)
    vmem = pl.BlockSpec(memory_space=pltpu.VMEM)
    return call(
        functools.partial(grad_kernel, stage, halo),
        [jax.ShapeDtypeStruct(total, F32)] * 2,
        in_specs=[pl.BlockSpec(memory_space=pltpu.SMEM)] + [vmem] * (len(inputs) - 1),
        scratch_shapes=[pltpu.VMEM(total, BF16)] * 2,
        mib=24,
        flops=COST,
    )(*inputs)


COST = 4 * 10**9


def place_kernel(mine, other, out_ref):
    _, _, core = place()
    for part in range(PARTS):
        for kind in range(2):
            cols = pl.ds((part * 2 + kind) * HD, HD)
            for half in range(2):
                total = jnp.where(core == half, mine[:, cols], other[:, cols].astype(F32))
                out_ref[0, :, pl.ds((kind * KVH + half * PARTS + part) * HD, HD)] = total.astype(out_ref.dtype)


def on_device(queries, stash, grad_out, lengths):
    rows = queries.shape[1]
    pipe, ctx = lax.axis_size("pipe"), lax.axis_size("ctx")
    halo = -(-lengths.shape[0] // 16) * 16
    high = 1 << (pipe.bit_length() - 2)

    def pairs(pick):
        return [(c, (c + pick[c % GROUP]) % ctx) for c in range(ctx)]

    def partner(block, pick):
        route = [((p ^ high) * ctx + c, p * ctx + d) for p in range(pipe) for c, d in pairs(pick)]
        return lax.ppermute(block, ("pipe", "ctx"), route)

    def along(block, pick):
        return lax.ppermute(block, "ctx", pairs(pick))

    stay = (0,) * GROUP
    flip = [tuple((rank ^ step) - rank for rank in range(GROUP)) for step in range(GROUP)]

    def shape(*dims):
        return jax.ShapeDtypeStruct(dims, BF16)

    def after(value, *others):
        return lax.optimization_barrier((value, *others))[0]

    edge_wide = 2 * PARTS * HD
    hbm = pl.BlockSpec(memory_space=pltpu.HBM)
    held = partner(stash, stay)

    wide = PARTS * WIDE
    size = edge_rows(lengths.shape[0])

    def beside(queries, grad_out):
        far, edge0, edge1 = call(
            functools.partial(hand_kernel, halo, lengths.shape[0]),
            [shape(2 * rows, wide), *[shape(2 * PARTS * size, HD)] * 2],
            in_specs=[hbm] * 2,
            scratch_shapes=[pltpu.VMEM((halo, 2 * wide), BF16)] * 2 + [pltpu.SemaphoreType.DMA((4,))],
        )(queries, grad_out)
        return along(far, flip[1]), along(edge0, (-4, -4, 4, 4)), along(edge1, (-3, -5, 5, 3))

    def nothing(*_):
        return jnp.zeros((2 * rows, wide), BF16), *[jnp.zeros((2 * PARTS * size, HD), BF16)] * 2

    far, edge0, edge1 = lax.cond(lengths[0] > 0, beside, nothing, queries, grad_out)
    q_buf, g_buf = call(
        stage_kernel,
        [shape(PARTS, 2 * WIDE + size, HD)] * 2,
        in_specs=[hbm] * 5,
        scratch_shapes=[pltpu.SemaphoreType.DMA((4 * PARTS * SHARE + 2 * PARTS,))],
    )(queries, grad_out, far, edge0, edge1)
    held, q_buf, g_buf = lax.optimization_barrier((held, q_buf, g_buf))
    far, *parts = call(split_kernel, [shape(rows, edge_wide), *[shape(rows, 2 * HD)] * (2 * PARTS)])(held)
    owns, fars = parts[:PARTS], parts[PARTS:]

    one = along(far, flip[1])
    got = [(own, one, along(own, flip[2]), along(far, flip[3])) for own, far in zip(owns, fars)]
    edge = call(edge_kernel, shape(halo, edge_wide))(*owns, one)
    edges = along(edge, (2, 2, 2, 2)), along(edge, (-4, -4, 4, 4))
    raw = grads(0, halo, rows, lengths, q_buf, g_buf, *got[0], *owns[1:], *edges)
    first = call(functools.partial(across_kernel, 0, halo), shape(rows + halo, edge_wide))(*raw)
    first = along(first, flip[2])
    raw = grads(1, halo, rows, lengths, q_buf, g_buf, *raw, *got[1], *edges)
    second = along(call(functools.partial(across_kernel, 1, halo), shape(rows, edge_wide))(*raw), flip[2])
    ends = along(call(functools.partial(ends_kernel, halo), shape(halo, edge_wide))(*raw, first), (4, 4, -4, -4))
    mine, other = call(
        join_kernel, [jax.ShapeDtypeStruct((rows, edge_wide), F32), shape(rows, edge_wide)]
    )(*raw, first, second, ends)
    return call(place_kernel, shape(1, rows, 2 * KVH * HD))(mine, along(other, flip[1]))


def solution(mesh):
    placed = (P("pipe", "ctx", None), P("pipe", "ctx", None), P("pipe", "ctx", None), P())
    return jax.shard_map(
        on_device, mesh=mesh, in_specs=placed, out_specs=P("pipe", "ctx", None), check_vma=False
    )
```

```python
import functools
import math

import jax
import jax.numpy as jnp
from jax import lax
from jax.experimental import pallas as pl
from jax.experimental.pallas import tpu as pltpu
from jax.sharding import PartitionSpec as P

H = 32
KVH = 4
HD = 128
REACH = 5
GROUP = REACH - 1
SHARE = H // KVH
PARTS = KVH // 2
WIDE = SHARE * HD
MASKED = -1e30
F32 = jnp.float32
BF16 = jnp.bfloat16
NT = (((1,), (1,)), ((), ()))
NN = (((1,), (0,)), ((), ()))


def place():
    me = lax.axis_index("ctx")
    rank = lax.rem(me, GROUP)
    return me, rank, lax.rem(rank, 2)


def call(body, out, mib=8, flops=1000, **more):
    return pl.pallas_call(
        body,
        out_shape=out,
        compiler_params=pltpu.CompilerParams(vmem_limit_bytes=mib * 2**20),
        cost_estimate=pl.CostEstimate(flops=flops, bytes_accessed=1000, transcendentals=0),
        **more,
    )


def columns(head):
    return pl.ds(pl.multiple_of(head * HD, HD), HD)


def split_kernel(kv_ref, far, *parts):
    _, _, core = place()
    for half, refs in ((core, parts[:PARTS]), (1 - core, parts[PARTS:])):
        for part, ref in enumerate(refs):
            for kind in range(2):
                block = kv_ref[0, :, columns(half * PARTS + part + kind * KVH)]
                ref[:, pl.ds(kind * HD, HD)] = block
                if half is not core:
                    far[:, pl.ds((part * 2 + kind) * HD, HD)] = block


def edge_rows(docs):
    return -(-SHARE * docs // 16) * 16


def hand_kernel(halo, docs, q_ref, g_ref, far, edge0, edge1, q_top, g_top, sem):
    _, _, core = place()
    rows = q_ref.shape[1]
    wide = PARTS * WIDE
    start = pl.multiple_of((1 - core) * wide, wide)
    tops = [(ref.at[0, pl.ds(0, halo)], top) for ref, top in ((q_ref, q_top), (g_ref, g_top))]
    whole = [
        (ref.at[0, :, pl.ds(start, wide)], far.at[pl.ds(at * rows, rows)]) for at, ref in enumerate((q_ref, g_ref))
    ]
    copies = [pltpu.make_async_copy(*copy, sem.at[at]) for at, copy in enumerate(tops + whole)]
    for copy in copies:
        copy.start()
    size = edge_rows(docs)
    to = lax.broadcasted_iota(jnp.int32, (size, SHARE * halo), 0)
    at = lax.broadcasted_iota(jnp.int32, (size, SHARE * halo), 1)
    picked = ((at // halo == to // docs) & (at % halo == to % docs)).astype(BF16)
    for copy in copies[:2]:
        copy.wait()
    for kind, top in enumerate((q_top, g_top)):
        for half, edge in enumerate((edge0, edge1)):
            for part in range(PARTS):
                heads = [(half * PARTS + part) * SHARE + head for head in range(SHARE)]
                block = jnp.concatenate([top[:, pl.ds(head * HD, HD)] for head in heads], axis=0)
                chosen = lax.dot_general(picked, block, NN, preferred_element_type=F32).astype(BF16)
                edge[pl.ds((kind * PARTS + part) * size, size), :] = chosen
    for copy in copies[2:]:
        copy.wait()


def edge_kernel(*refs):
    *own, one, edge = refs
    _, rank, _ = place()
    halo = edge.shape[0]
    first = pl.ds(pl.multiple_of(jnp.where(rank < 2, 0, one.shape[0] - halo), 16), halo)
    for part, ref in enumerate(own):
        cols = pl.ds(part * 2 * HD, 2 * HD)
        edge[:, cols] = jnp.where((rank == 0) | (rank == GROUP - 1), ref[first, :], one[first, cols])


def stage_kernel(q_ref, g_ref, far, edge0, edge1, q_buf, g_buf, sem):
    _, _, core = place()
    rows = q_ref.shape[1]
    copies = []
    for kind, (ref, buf) in enumerate(((q_ref, q_buf), (g_ref, g_buf))):
        for part in range(PARTS):
            for head in range(SHARE):
                here = head * rows
                mine = ref.at[0, :, columns((core * PARTS + part) * SHARE + head)]
                other = far.at[pl.ds(kind * rows, rows), pl.ds((part * SHARE + head) * HD, HD)]
                for slot, block in ((core, mine), (1 - core, other)):
                    at = pl.ds(pl.multiple_of(slot * WIDE + here, 16), rows)
                    copies.append((block, buf.at[part, at]))
    copies = [pltpu.make_async_copy(*copy, sem.at[at]) for at, copy in enumerate(copies)]
    for copy in copies:
        copy.start()
    size = edge0.shape[0] // (2 * PARTS)
    for half, edge in enumerate((edge0, edge1)):

        @pl.when(core == half)
        def _():
            extra = []
            for kind, buf in enumerate((q_buf, g_buf)):
                for part in range(PARTS):
                    block = edge.at[pl.ds((kind * PARTS + part) * size, size)]
                    to = buf.at[part, pl.ds(2 * WIDE, size)]
                    extra.append(pltpu.make_async_copy(block, to, sem.at[len(copies) + len(extra)]))
            for copy in extra:
                copy.start()
            for copy in extra:
                copy.wait()

    for copy in copies:
        copy.wait()


def doc_start(pos, len_ref):
    start = jnp.zeros_like(pos)
    end = jnp.int32(0)
    for doc in range(len_ref.shape[0]):
        end = end + len_ref[doc]
        start = jnp.where(end <= pos, end, start)
    return start


def bias_of(first_key, keys, query_pos, start):
    key_pos = first_key + lax.broadcasted_iota(jnp.int32, (keys, query_pos.shape[1]), 0)
    return jnp.where((key_pos >= start) & (key_pos <= query_pos), 0.0, MASKED)


def raise_scores(key, query, bias):
    return lax.dot_general(key, query, NT, preferred_element_type=F32) + bias


def softmax(scores, keep):
    top = jnp.max(scores, axis=0, keepdims=True)
    raw = jnp.exp2((scores - top) * (HD**-0.5 * math.log2(math.e)))
    return raw * (keep / jnp.sum(raw, axis=0, keepdims=True))


def grad_kernel(stage, halo, len_ref, q_buf, g_buf, *refs):
    if stage:
        dk_last, dv_last, *refs = refs
    *got, edge_a, edge_b, dk_ref, dv_ref, k_buf, v_buf = refs
    rows = got[0].shape[0]
    span = GROUP * rows
    me, rank, _ = place()
    first = (me - rank) * rows
    docs = len_ref.shape[0]

    def load(part, blocks):
        here = pl.ds(part * 2 * HD, 2 * HD)
        low, high = jnp.where(rank < 2, edge_a[:, here], edge_b[:, here]), edge_b[:, here]
        for buf, kind in ((k_buf, 0), (v_buf, HD)):
            for step, block in enumerate(blocks):
                at = pl.ds(pl.multiple_of(halo + (rank ^ step) * rows, 16), rows)
                buf[part, at, :] = block[:, kind : kind + HD]
            buf[part, :halo, :] = low[:, kind : kind + HD]
            buf[part, halo + span :, :] = high[:, kind : kind + HD]

    own, one, two, three = got[:4]
    here = pl.ds(stage * 2 * HD, 2 * HD)
    load(stage, (own[...], one[:, here], two[...], three[...]))
    if stage:
        dk_ref[...] = dk_last[...]
        dv_ref[...] = dv_last[...]
    else:
        for part, own in enumerate(got[4:], 1):
            load(part, (own[...], one[:, pl.ds(part * 2 * HD, 2 * HD)]))
        dk_ref[...] = jnp.zeros_like(dk_ref)
        dv_ref[...] = jnp.zeros_like(dv_ref)

    for chip in range(2):

        @pl.when(rank // 2 == chip)
        def _():
            tiles = []
            for part in (stage,) if chip else range(0 if stage == 0 else PARTS, PARTS):
                for slot in range(2):
                    block = 2 * chip + slot
                    query_pos = first + block * rows + lax.broadcasted_iota(jnp.int32, (1, rows), 1)
                    start = doc_start(query_pos, len_ref)
                    keep = jnp.where(start < first - halo, 0.0, 1.0)
                    tiles.append((part, pl.ds(slot * WIDE, WIDE), 0, halo + (block + 1) * rows, query_pos, start, keep, SHARE))
            if chip == 0:
                size = edge_rows(docs)
                lane = lax.broadcasted_iota(jnp.int32, (1, size), 1)
                query_pos = first + span + lax.rem(lane, docs)
                start = doc_start(query_pos, len_ref)
                keep = jnp.where((start < first + span - halo) & (lane < SHARE * docs), 1.0, 0.0)
                tiles.append((stage, pl.ds(2 * WIDE, size), halo, halo + span + halo, query_pos, start, keep, 1))
            def raised(tile):
                part, cols, low, high, query_pos, start, keep, times = tile
                bias = bias_of(first - halo + low, high - low, query_pos, start)
                bias = jnp.concatenate([bias] * times, axis=1)
                return raise_scores(k_buf[part, pl.ds(low, high - low), :], q_buf[part, cols, :], bias)

            scores = raised(tiles[0])
            for at, (part, cols, low, high, query_pos, start, keep, times) in enumerate(tiles):
                keys = pl.ds(low, high - low)
                query, cot = q_buf[part, cols, :], g_buf[part, cols, :]
                weights = softmax(scores, jnp.concatenate([keep] * times, axis=1))
                dweights = lax.dot_general(v_buf[part, keys, :], cot, NT, preferred_element_type=F32)
                dv_ref[part, keys, :] += lax.dot_general(weights.astype(BF16), cot, NN, preferred_element_type=F32)
                if at + 1 < len(tiles):
                    scores = raised(tiles[at + 1])
                delta = jnp.sum(weights * dweights, axis=0, keepdims=True)
                dscores = (weights * (dweights - delta)).astype(BF16)
                dk_ref[part, keys, :] += lax.dot_general(dscores, query, NN, preferred_element_type=F32)


def terms(dk_ref, dv_ref, part, row, size):
    at = pl.ds(row if isinstance(row, int) else pl.multiple_of(row, 16), size)
    return jnp.concatenate([dk_ref[part, at, :] * HD**-0.5, dv_ref[part, at, :]], axis=1)


def across_kernel(part, halo, dk_ref, dv_ref, across):
    _, rank, _ = place()
    kv = 2 * HD
    rows = across.shape[0] - (0 if part else halo)
    for which in range(PARTS):
        cols = pl.ds(which * kv, kv)
        across[:rows, cols] = terms(dk_ref, dv_ref, part, halo + (rank ^ (2 + which)) * rows, rows).astype(BF16)
        if not part:
            across[rows:, cols] = terms(dk_ref, dv_ref, which, 0, halo).astype(BF16)


def ends_kernel(halo, dk_ref, dv_ref, across, ends):
    _, rank, _ = place()
    kv = 2 * HD
    rows = across.shape[0] - halo
    for part in range(PARTS):
        cols = pl.ds(part * kv, kv)
        before = terms(dk_ref, dv_ref, part, 0, halo) + across[rows:, cols].astype(F32)
        behind = terms(dk_ref, dv_ref, part, halo + GROUP * rows, halo)
        ends[:, cols] = jnp.where(rank < 2, behind, before).astype(BF16)


def join_kernel(dk_ref, dv_ref, across0, across1, ends, mine, other):
    kv = 2 * HD
    halo, (rows, _) = ends.shape[0], mine.shape
    _, rank, _ = place()
    for ref, step, first, last in ((mine, 0, 0, GROUP - 1), (other, 1, 1, GROUP - 2)):
        for part, across in enumerate((across0, across1)):
            cols = pl.ds(part * kv, kv)
            total = terms(dk_ref, dv_ref, part, halo + (rank ^ step) * rows, rows)
            total = total + across[:rows, pl.ds(step * kv, kv)].astype(F32)
            end = ends[:, cols].astype(F32)
            low = total[:halo] + jnp.where(rank == first, end, 0.0)
            high = total[rows - halo :] + jnp.where(rank == last, end, 0.0)
            ref[:, cols] = jnp.concatenate([low, total[halo : rows - halo], high], axis=0).astype(ref.dtype)


def grads(stage, halo, rows, *inputs):
    total = (PARTS, halo + GROUP * rows + halo, HD)
    vmem = pl.BlockSpec(memory_space=pltpu.VMEM)
    return call(
        functools.partial(grad_kernel, stage, halo),
        [jax.ShapeDtypeStruct(total, F32)] * 2,
        in_specs=[pl.BlockSpec(memory_space=pltpu.SMEM)] + [vmem] * (len(inputs) - 1),
        scratch_shapes=[pltpu.VMEM(total, BF16)] * 2,
        mib=24,
        flops=COST,
    )(*inputs)


COST = 4 * 10**9


def place_kernel(other, block, *refs):
    *_, out_ref, heads, sem = refs
    _, _, core = place()
    half = 1 - core if other else core
    copies = []
    for kind in range(2):
        for part in range(PARTS):
            to = (kind * PARTS + part) * HD
            heads[:, to : to + HD] = block[:, pl.ds((part * 2 + kind) * HD, HD)].astype(BF16)
        wide = PARTS * HD
        to = pl.ds(pl.multiple_of((kind * KVH + half * PARTS) * HD, HD), wide)
        copies.append(pltpu.make_async_copy(heads.at[:, pl.ds(kind * wide, wide)], out_ref.at[0, :, to], sem.at[kind]))
        copies[-1].start()
    for copy in copies:
        copy.wait()


def on_device(queries, stash, grad_out, lengths):
    rows = queries.shape[1]
    pipe, ctx = lax.axis_size("pipe"), lax.axis_size("ctx")
    halo = -(-lengths.shape[0] // 16) * 16
    high = 1 << (pipe.bit_length() - 2)

    def pairs(pick):
        return [(c, (c + pick[c % GROUP]) % ctx) for c in range(ctx)]

    def partner(block, pick):
        route = [((p ^ high) * ctx + c, p * ctx + d) for p in range(pipe) for c, d in pairs(pick)]
        return lax.ppermute(block, ("pipe", "ctx"), route)

    def along(block, pick):
        return lax.ppermute(block, "ctx", pairs(pick))

    stay = (0,) * GROUP
    flip = [tuple((rank ^ step) - rank for rank in range(GROUP)) for step in range(GROUP)]

    def shape(*dims):
        return jax.ShapeDtypeStruct(dims, BF16)

    def after(value, *others):
        return lax.optimization_barrier((value, *others))[0]

    edge_wide = 2 * PARTS * HD
    hbm = pl.BlockSpec(memory_space=pltpu.HBM)
    held = partner(stash, stay)

    wide = PARTS * WIDE
    size = edge_rows(lengths.shape[0])

    def beside(queries, grad_out):
        far, edge0, edge1 = call(
            functools.partial(hand_kernel, halo, lengths.shape[0]),
            [shape(2 * rows, wide), *[shape(2 * PARTS * size, HD)] * 2],
            in_specs=[hbm] * 2,
            scratch_shapes=[pltpu.VMEM((halo, 2 * wide), BF16)] * 2 + [pltpu.SemaphoreType.DMA((4,))],
        )(queries, grad_out)
        return along(far, flip[1]), along(edge0, (-4, -4, 4, 4)), along(edge1, (-3, -5, 5, 3))

    def nothing(*_):
        return jnp.zeros((2 * rows, wide), BF16), *[jnp.zeros((2 * PARTS * size, HD), BF16)] * 2

    far, edge0, edge1 = lax.cond(lengths[0] > 0, beside, nothing, queries, grad_out)
    q_buf, g_buf = call(
        stage_kernel,
        [shape(PARTS, 2 * WIDE + size, HD)] * 2,
        in_specs=[hbm] * 5,
        scratch_shapes=[pltpu.SemaphoreType.DMA((4 * PARTS * SHARE + 2 * PARTS,))],
    )(queries, grad_out, far, edge0, edge1)
    held, q_buf, g_buf = lax.optimization_barrier((held, q_buf, g_buf))
    far, *parts = call(split_kernel, [shape(rows, edge_wide), *[shape(rows, 2 * HD)] * (2 * PARTS)])(held)
    owns, fars = parts[:PARTS], parts[PARTS:]

    one = along(far, flip[1])
    got = [(own, one, along(own, flip[2]), along(far, flip[3])) for own, far in zip(owns, fars)]
    edge = call(edge_kernel, shape(halo, edge_wide))(*owns, one)
    edges = along(edge, (2, 2, 2, 2)), along(edge, (-4, -4, 4, 4))
    raw = grads(0, halo, rows, lengths, q_buf, g_buf, *got[0], *owns[1:], *edges)
    first = call(functools.partial(across_kernel, 0, halo), shape(rows + halo, edge_wide))(*raw)
    first = along(first, flip[2])
    raw = grads(1, halo, rows, lengths, q_buf, g_buf, *raw, *got[1], *edges)
    second = along(call(functools.partial(across_kernel, 1, halo), shape(rows, edge_wide))(*raw), flip[2])
    ends = along(call(functools.partial(ends_kernel, halo), shape(halo, edge_wide))(*raw, first), (4, 4, -4, -4))
    mine, other = call(
        join_kernel, [jax.ShapeDtypeStruct((rows, edge_wide), F32), shape(rows, edge_wide)]
    )(*raw, first, second, ends)
    vmem = pl.BlockSpec(memory_space=pltpu.VMEM)
    settle = dict(
        out=shape(1, rows, 2 * KVH * HD),
        out_specs=hbm,
        scratch_shapes=[pltpu.VMEM((rows, edge_wide), BF16), pltpu.SemaphoreType.DMA((2,))],
    )
    out = call(functools.partial(place_kernel, False), in_specs=[vmem], **settle)(mine)
    return call(
        functools.partial(place_kernel, True), in_specs=[vmem, hbm], input_output_aliases={1: 0}, **settle
    )(along(other, flip[1]), out)


def solution(mesh):
    placed = (P("pipe", "ctx", None), P("pipe", "ctx", None), P("pipe", "ctx", None), P())
    return jax.shard_map(
        on_device, mesh=mesh, in_specs=placed, out_specs=P("pipe", "ctx", None), check_vma=False
    )
```

```python
import functools
import math

import jax
import jax.numpy as jnp
from jax import lax
from jax.experimental import pallas as pl
from jax.experimental.pallas import tpu as pltpu
from jax.sharding import PartitionSpec as P

H = 32
KVH = 4
HD = 128
REACH = 5
GROUP = REACH - 1
SHARE = H // KVH
PARTS = KVH // 2
WIDE = SHARE * HD
MASKED = -1e30
F32 = jnp.float32
BF16 = jnp.bfloat16
NT = (((1,), (1,)), ((), ()))
NN = (((1,), (0,)), ((), ()))


def place():
    me = lax.axis_index("ctx")
    rank = lax.rem(me, GROUP)
    return me, rank, lax.rem(rank, 2)


def call(body, out, mib=8, flops=1000, **more):
    return pl.pallas_call(
        body,
        out_shape=out,
        compiler_params=pltpu.CompilerParams(vmem_limit_bytes=mib * 2**20),
        cost_estimate=pl.CostEstimate(flops=flops, bytes_accessed=1000, transcendentals=0),
        **more,
    )


def columns(head):
    return pl.ds(pl.multiple_of(head * HD, HD), HD)


def split_kernel(kv_ref, far, *parts):
    _, _, core = place()
    for half, refs in ((core, parts[:PARTS]), (1 - core, parts[PARTS:])):
        for part, ref in enumerate(refs):
            for kind in range(2):
                block = kv_ref[0, :, columns(half * PARTS + part + kind * KVH)]
                ref[:, pl.ds(kind * HD, HD)] = block
                if half is not core:
                    far[:, pl.ds((part * 2 + kind) * HD, HD)] = block


def edge_rows(docs):
    return -(-SHARE * docs // 16) * 16


def hand_kernel(halo, docs, q_ref, g_ref, far, edge0, edge1, q_top, g_top, sem):
    _, _, core = place()
    rows = q_ref.shape[1]
    wide = PARTS * WIDE
    start = pl.multiple_of((1 - core) * wide, wide)
    tops = [(ref.at[0, pl.ds(0, halo)], top) for ref, top in ((q_ref, q_top), (g_ref, g_top))]
    whole = [
        (ref.at[0, :, pl.ds(start, wide)], far.at[pl.ds(at * rows, rows)]) for at, ref in enumerate((q_ref, g_ref))
    ]
    copies = [pltpu.make_async_copy(*copy, sem.at[at]) for at, copy in enumerate(tops + whole)]
    for copy in copies:
        copy.start()
    size = edge_rows(docs)
    to = lax.broadcasted_iota(jnp.int32, (size, SHARE * halo), 0)
    at = lax.broadcasted_iota(jnp.int32, (size, SHARE * halo), 1)
    picked = ((at // halo == to // docs) & (at % halo == to % docs)).astype(BF16)
    for copy in copies[:2]:
        copy.wait()
    for kind, top in enumerate((q_top, g_top)):
        for half, edge in enumerate((edge0, edge1)):
            for part in range(PARTS):
                heads = [(half * PARTS + part) * SHARE + head for head in range(SHARE)]
                block = jnp.concatenate([top[:, pl.ds(head * HD, HD)] for head in heads], axis=0)
                chosen = lax.dot_general(picked, block, NN, preferred_element_type=F32).astype(BF16)
                edge[pl.ds((kind * PARTS + part) * size, size), :] = chosen
    for copy in copies[2:]:
        copy.wait()


def edge_kernel(*refs):
    *own, one, edge = refs
    _, rank, _ = place()
    halo = edge.shape[0]
    first = pl.ds(pl.multiple_of(jnp.where(rank < 2, 0, one.shape[0] - halo), 16), halo)
    for part, ref in enumerate(own):
        cols = pl.ds(part * 2 * HD, 2 * HD)
        edge[:, cols] = jnp.where((rank == 0) | (rank == GROUP - 1), ref[first, :], one[first, cols])


def stage_kernel(q_ref, g_ref, far, edge0, edge1, q_buf, g_buf, sem):
    _, _, core = place()
    rows = q_ref.shape[1]
    copies = []
    for kind, (ref, buf) in enumerate(((q_ref, q_buf), (g_ref, g_buf))):
        for part in range(PARTS):
            for head in range(SHARE):
                here = head * rows
                mine = ref.at[0, :, columns((core * PARTS + part) * SHARE + head)]
                other = far.at[pl.ds(kind * rows, rows), pl.ds((part * SHARE + head) * HD, HD)]
                for slot, block in ((core, mine), (1 - core, other)):
                    at = pl.ds(pl.multiple_of(slot * WIDE + here, 16), rows)
                    copies.append((block, buf.at[part, at]))
    copies = [pltpu.make_async_copy(*copy, sem.at[at]) for at, copy in enumerate(copies)]
    for copy in copies:
        copy.start()
    size = edge0.shape[0] // (2 * PARTS)
    for half, edge in enumerate((edge0, edge1)):

        @pl.when(core == half)
        def _():
            extra = []
            for kind, buf in enumerate((q_buf, g_buf)):
                for part in range(PARTS):
                    block = edge.at[pl.ds((kind * PARTS + part) * size, size)]
                    to = buf.at[part, pl.ds(2 * WIDE, size)]
                    extra.append(pltpu.make_async_copy(block, to, sem.at[len(copies) + len(extra)]))
            for copy in extra:
                copy.start()
            for copy in extra:
                copy.wait()

    for copy in copies:
        copy.wait()


def doc_start(pos, len_ref):
    start = jnp.zeros_like(pos)
    end = jnp.int32(0)
    for doc in range(len_ref.shape[0]):
        end = end + len_ref[doc]
        start = jnp.where(end <= pos, end, start)
    return start


def bias_of(first_key, keys, query_pos, start):
    key_pos = first_key + lax.broadcasted_iota(jnp.int32, (keys, query_pos.shape[1]), 0)
    return jnp.where((key_pos >= start) & (key_pos <= query_pos), 0.0, MASKED)


def raise_scores(key, query, bias):
    return lax.dot_general(key, query, NT, preferred_element_type=F32) + bias


def softmax(scores, keep):
    top = jnp.max(scores, axis=0, keepdims=True)
    raw = jnp.exp2((scores - top) * (HD**-0.5 * math.log2(math.e)))
    return raw * (keep / jnp.sum(raw, axis=0, keepdims=True))


def grad_kernel(stage, halo, len_ref, q_buf, g_buf, *refs):
    if stage:
        dk_last, dv_last, *refs = refs
    *got, edge_a, edge_b, dk_ref, dv_ref, k_buf, v_buf = refs
    rows = got[0].shape[0]
    span = GROUP * rows
    me, rank, _ = place()
    first = (me - rank) * rows
    docs = len_ref.shape[0]

    def load(part, blocks):
        here = pl.ds(part * 2 * HD, 2 * HD)
        low, high = jnp.where(rank < 2, edge_a[:, here], edge_b[:, here]), edge_b[:, here]
        for buf, kind in ((k_buf, 0), (v_buf, HD)):
            for step, block in enumerate(blocks):
                at = pl.ds(pl.multiple_of(halo + (rank ^ step) * rows, 16), rows)
                buf[part, at, :] = block[:, kind : kind + HD]
            buf[part, :halo, :] = low[:, kind : kind + HD]
            buf[part, halo + span :, :] = high[:, kind : kind + HD]

    own, one, two, three = got[:4]
    here = pl.ds(stage * 2 * HD, 2 * HD)
    load(stage, (own[...], one[:, here], two[...], three[...]))
    if stage:
        dk_ref[...] = dk_last[...]
        dv_ref[...] = dv_last[...]
    else:
        for part, own in enumerate(got[4:], 1):
            load(part, (own[...], one[:, pl.ds(part * 2 * HD, 2 * HD)]))
        dk_ref[...] = jnp.zeros_like(dk_ref)
        dv_ref[...] = jnp.zeros_like(dv_ref)

    for chip in range(2):

        @pl.when(rank // 2 == chip)
        def _():
            tiles = []
            for part in (stage,) if chip else range(0 if stage == 0 else PARTS, PARTS):
                for slot in range(2):
                    block = 2 * chip + slot
                    query_pos = first + block * rows + lax.broadcasted_iota(jnp.int32, (1, rows), 1)
                    start = doc_start(query_pos, len_ref)
                    keep = jnp.where(start < first - halo, 0.0, 1.0)
                    tiles.append((part, pl.ds(slot * WIDE, WIDE), 0, halo + (block + 1) * rows, query_pos, start, keep, SHARE))
            if chip == 0:
                size = edge_rows(docs)
                lane = lax.broadcasted_iota(jnp.int32, (1, size), 1)
                query_pos = first + span + lax.rem(lane, docs)
                start = doc_start(query_pos, len_ref)
                keep = jnp.where((start < first + span - halo) & (lane < SHARE * docs), 1.0, 0.0)
                tiles.append((stage, pl.ds(2 * WIDE, size), halo, halo + span + halo, query_pos, start, keep, 1))
            def raised(tile):
                part, cols, low, high, query_pos, start, keep, times = tile
                bias = bias_of(first - halo + low, high - low, query_pos, start)
                bias = jnp.concatenate([bias] * times, axis=1)
                return raise_scores(k_buf[part, pl.ds(low, high - low), :], q_buf[part, cols, :], bias)

            tiles.reverse()
            scores = raised(tiles[0])
            for at, (part, cols, low, high, query_pos, start, keep, times) in enumerate(tiles):
                keys = pl.ds(low, high - low)
                query, cot = q_buf[part, cols, :], g_buf[part, cols, :]
                weights = softmax(scores, jnp.concatenate([keep] * times, axis=1))
                dweights = lax.dot_general(v_buf[part, keys, :], cot, NT, preferred_element_type=F32)
                dv_ref[part, keys, :] += lax.dot_general(weights.astype(BF16), cot, NN, preferred_element_type=F32)
                if at + 1 < len(tiles):
                    scores = raised(tiles[at + 1])
                delta = jnp.sum(weights * dweights, axis=0, keepdims=True)
                dscores = (weights * (dweights - delta)).astype(BF16)
                dk_ref[part, keys, :] += lax.dot_general(dscores, query, NN, preferred_element_type=F32)


def terms(dk_ref, dv_ref, part, row, size):
    at = pl.ds(row if isinstance(row, int) else pl.multiple_of(row, 16), size)
    return jnp.concatenate([dk_ref[part, at, :] * HD**-0.5, dv_ref[part, at, :]], axis=1)


def across_kernel(part, halo, dk_ref, dv_ref, across):
    _, rank, _ = place()
    kv = 2 * HD
    rows = across.shape[0] - (0 if part else halo)
    for which in range(PARTS):
        cols = pl.ds(which * kv, kv)
        across[:rows, cols] = terms(dk_ref, dv_ref, part, halo + (rank ^ (2 + which)) * rows, rows).astype(BF16)
        if not part:
            across[rows:, cols] = terms(dk_ref, dv_ref, which, 0, halo).astype(BF16)


def ends_kernel(halo, dk_ref, dv_ref, across, ends):
    _, rank, _ = place()
    kv = 2 * HD
    rows = across.shape[0] - halo
    for part in range(PARTS):
        cols = pl.ds(part * kv, kv)
        before = terms(dk_ref, dv_ref, part, 0, halo) + across[rows:, cols].astype(F32)
        behind = terms(dk_ref, dv_ref, part, halo + GROUP * rows, halo)
        ends[:, cols] = jnp.where(rank < 2, behind, before).astype(BF16)


def join_kernel(dk_ref, dv_ref, across0, across1, ends, mine, other):
    kv = 2 * HD
    halo, (rows, _) = ends.shape[0], mine.shape
    _, rank, _ = place()
    for ref, step, first, last in ((mine, 0, 0, GROUP - 1), (other, 1, 1, GROUP - 2)):
        for part, across in enumerate((across0, across1)):
            cols = pl.ds(part * kv, kv)
            total = terms(dk_ref, dv_ref, part, halo + (rank ^ step) * rows, rows)
            total = total + across[:rows, pl.ds(step * kv, kv)].astype(F32)
            end = ends[:, cols].astype(F32)
            low = total[:halo] + jnp.where(rank == first, end, 0.0)
            high = total[rows - halo :] + jnp.where(rank == last, end, 0.0)
            ref[:, cols] = jnp.concatenate([low, total[halo : rows - halo], high], axis=0).astype(ref.dtype)


def grads(stage, halo, rows, *inputs):
    total = (PARTS, halo + GROUP * rows + halo, HD)
    vmem = pl.BlockSpec(memory_space=pltpu.VMEM)
    return call(
        functools.partial(grad_kernel, stage, halo),
        [jax.ShapeDtypeStruct(total, F32)] * 2,
        in_specs=[pl.BlockSpec(memory_space=pltpu.SMEM)] + [vmem] * (len(inputs) - 1),
        scratch_shapes=[pltpu.VMEM(total, BF16)] * 2,
        mib=24,
        flops=COST,
    )(*inputs)


COST = 4 * 10**9


def place_kernel(other, block, *refs):
    *_, out_ref, heads, sem = refs
    _, _, core = place()
    half = 1 - core if other else core
    copies = []
    for kind in range(2):
        for part in range(PARTS):
            to = (kind * PARTS + part) * HD
            heads[:, to : to + HD] = block[:, pl.ds((part * 2 + kind) * HD, HD)].astype(BF16)
        wide = PARTS * HD
        to = pl.ds(pl.multiple_of((kind * KVH + half * PARTS) * HD, HD), wide)
        copies.append(pltpu.make_async_copy(heads.at[:, pl.ds(kind * wide, wide)], out_ref.at[0, :, to], sem.at[kind]))
        copies[-1].start()
    for copy in copies:
        copy.wait()


def on_device(queries, stash, grad_out, lengths):
    rows = queries.shape[1]
    pipe, ctx = lax.axis_size("pipe"), lax.axis_size("ctx")
    halo = -(-lengths.shape[0] // 16) * 16
    high = 1 << (pipe.bit_length() - 2)

    def pairs(pick):
        return [(c, (c + pick[c % GROUP]) % ctx) for c in range(ctx)]

    def partner(block, pick):
        route = [((p ^ high) * ctx + c, p * ctx + d) for p in range(pipe) for c, d in pairs(pick)]
        return lax.ppermute(block, ("pipe", "ctx"), route)

    def along(block, pick):
        return lax.ppermute(block, "ctx", pairs(pick))

    stay = (0,) * GROUP
    flip = [tuple((rank ^ step) - rank for rank in range(GROUP)) for step in range(GROUP)]

    def shape(*dims):
        return jax.ShapeDtypeStruct(dims, BF16)

    def after(value, *others):
        return lax.optimization_barrier((value, *others))[0]

    edge_wide = 2 * PARTS * HD
    hbm = pl.BlockSpec(memory_space=pltpu.HBM)
    held = partner(stash, stay)

    wide = PARTS * WIDE
    size = edge_rows(lengths.shape[0])

    def beside(queries, grad_out):
        far, edge0, edge1 = call(
            functools.partial(hand_kernel, halo, lengths.shape[0]),
            [shape(2 * rows, wide), *[shape(2 * PARTS * size, HD)] * 2],
            in_specs=[hbm] * 2,
            scratch_shapes=[pltpu.VMEM((halo, 2 * wide), BF16)] * 2 + [pltpu.SemaphoreType.DMA((4,))],
        )(queries, grad_out)
        return along(far, flip[1]), along(edge0, (-4, -4, 4, 4)), along(edge1, (-3, -5, 5, 3))

    def nothing(*_):
        return jnp.zeros((2 * rows, wide), BF16), *[jnp.zeros((2 * PARTS * size, HD), BF16)] * 2

    far, edge0, edge1 = lax.cond(lengths[0] > 0, beside, nothing, queries, grad_out)
    q_buf, g_buf = call(
        stage_kernel,
        [shape(PARTS, 2 * WIDE + size, HD)] * 2,
        in_specs=[hbm] * 5,
        scratch_shapes=[pltpu.SemaphoreType.DMA((4 * PARTS * SHARE + 2 * PARTS,))],
    )(queries, grad_out, far, edge0, edge1)
    held, q_buf, g_buf = lax.optimization_barrier((held, q_buf, g_buf))
    far, *parts = call(split_kernel, [shape(rows, edge_wide), *[shape(rows, 2 * HD)] * (2 * PARTS)])(held)
    owns, fars = parts[:PARTS], parts[PARTS:]

    one = along(far, flip[1])
    got = [(own, one, along(own, flip[2]), along(far, flip[3])) for own, far in zip(owns, fars)]
    edge = call(edge_kernel, shape(halo, edge_wide))(*owns, one)
    edges = along(edge, (2, 2, 2, 2)), along(edge, (-4, -4, 4, 4))
    raw = grads(0, halo, rows, lengths, q_buf, g_buf, *got[0], *owns[1:], *edges)
    first = call(functools.partial(across_kernel, 0, halo), shape(rows + halo, edge_wide))(*raw)
    first = along(first, flip[2])
    raw = grads(1, halo, rows, lengths, q_buf, g_buf, *raw, *got[1], *edges)
    second = along(call(functools.partial(across_kernel, 1, halo), shape(rows, edge_wide))(*raw), flip[2])
    ends = along(call(functools.partial(ends_kernel, halo), shape(halo, edge_wide))(*raw, first), (4, 4, -4, -4))
    mine, other = call(
        join_kernel, [jax.ShapeDtypeStruct((rows, edge_wide), F32), shape(rows, edge_wide)]
    )(*raw, first, second, ends)
    vmem = pl.BlockSpec(memory_space=pltpu.VMEM)
    settle = dict(
        out=shape(1, rows, 2 * KVH * HD),
        out_specs=hbm,
        scratch_shapes=[pltpu.VMEM((rows, edge_wide), BF16), pltpu.SemaphoreType.DMA((2,))],
    )
    out = call(functools.partial(place_kernel, False), in_specs=[vmem], **settle)(mine)
    return call(
        functools.partial(place_kernel, True), in_specs=[vmem, hbm], input_output_aliases={1: 0}, **settle
    )(along(other, flip[1]), out)


def solution(mesh):
    placed = (P("pipe", "ctx", None), P("pipe", "ctx", None), P("pipe", "ctx", None), P())
    return jax.shard_map(
        on_device, mesh=mesh, in_specs=placed, out_specs=P("pipe", "ctx", None), check_vma=False
    )
```

```python
import functools
import math

import jax
import jax.numpy as jnp
from jax import lax
from jax.experimental import pallas as pl
from jax.experimental.pallas import tpu as pltpu
from jax.sharding import PartitionSpec as P

H = 32
KVH = 4
HD = 128
REACH = 5
GROUP = REACH - 1
SHARE = H // KVH
PARTS = KVH // 2
WIDE = SHARE * HD
MASKED = -1e30
F32 = jnp.float32
BF16 = jnp.bfloat16
NT = (((1,), (1,)), ((), ()))
NN = (((1,), (0,)), ((), ()))


def place():
    me = lax.axis_index("ctx")
    rank = lax.rem(me, GROUP)
    return me, rank, lax.rem(rank, 2)


def call(body, out, mib=8, flops=1000, **more):
    return pl.pallas_call(
        body,
        out_shape=out,
        compiler_params=pltpu.CompilerParams(vmem_limit_bytes=mib * 2**20),
        cost_estimate=pl.CostEstimate(flops=flops, bytes_accessed=1000, transcendentals=0),
        **more,
    )


def columns(head):
    return pl.ds(pl.multiple_of(head * HD, HD), HD)


def split_kernel(kv_ref, far, *parts):
    _, _, core = place()
    for half, refs in ((core, parts[:PARTS]), (1 - core, parts[PARTS:])):
        for part, ref in enumerate(refs):
            for kind in range(2):
                block = kv_ref[0, :, columns(half * PARTS + part + kind * KVH)]
                ref[:, pl.ds(kind * HD, HD)] = block
                if half is not core:
                    far[:, pl.ds((part * 2 + kind) * HD, HD)] = block


def edge_rows(docs):
    return -(-SHARE * docs // 16) * 16


def hand_kernel(halo, docs, q_ref, g_ref, far, edge0, edge1, q_top, g_top, sem):
    _, _, core = place()
    rows = q_ref.shape[1]
    wide = PARTS * WIDE
    start = pl.multiple_of((1 - core) * wide, wide)
    tops = [(ref.at[0, pl.ds(0, halo)], top) for ref, top in ((q_ref, q_top), (g_ref, g_top))]
    whole = [
        (ref.at[0, :, pl.ds(start, wide)], far.at[pl.ds(at * rows, rows)]) for at, ref in enumerate((q_ref, g_ref))
    ]
    copies = [pltpu.make_async_copy(*copy, sem.at[at]) for at, copy in enumerate(tops + whole)]
    for copy in copies:
        copy.start()
    size = edge_rows(docs)
    to = lax.broadcasted_iota(jnp.int32, (size, SHARE * halo), 0)
    at = lax.broadcasted_iota(jnp.int32, (size, SHARE * halo), 1)
    picked = ((at // halo == to // docs) & (at % halo == to % docs)).astype(BF16)
    for copy in copies[:2]:
        copy.wait()
    for kind, top in enumerate((q_top, g_top)):
        for half, edge in enumerate((edge0, edge1)):
            for part in range(PARTS):
                heads = [(half * PARTS + part) * SHARE + head for head in range(SHARE)]
                block = jnp.concatenate([top[:, pl.ds(head * HD, HD)] for head in heads], axis=0)
                chosen = lax.dot_general(picked, block, NN, preferred_element_type=F32).astype(BF16)
                edge[pl.ds((kind * PARTS + part) * size, size), :] = chosen
    for copy in copies[2:]:
        copy.wait()


def edge_kernel(*refs):
    *own, one, edge = refs
    _, rank, _ = place()
    halo = edge.shape[0]
    first = pl.ds(pl.multiple_of(jnp.where(rank < 2, 0, one.shape[0] - halo), 16), halo)
    for part, ref in enumerate(own):
        cols = pl.ds(part * 2 * HD, 2 * HD)
        edge[:, cols] = jnp.where((rank == 0) | (rank == GROUP - 1), ref[first, :], one[first, cols])


def stage_kernel(q_ref, g_ref, far, edge0, edge1, q_buf, g_buf, sem):
    _, _, core = place()
    rows = q_ref.shape[1]
    copies = []
    for kind, (ref, buf) in enumerate(((q_ref, q_buf), (g_ref, g_buf))):
        for part in range(PARTS):
            for head in range(SHARE):
                here = head * rows
                mine = ref.at[0, :, columns((core * PARTS + part) * SHARE + head)]
                other = far.at[pl.ds(kind * rows, rows), pl.ds((part * SHARE + head) * HD, HD)]
                for slot, block in ((core, mine), (1 - core, other)):
                    at = pl.ds(pl.multiple_of(slot * WIDE + here, 16), rows)
                    copies.append((block, buf.at[part, at]))
    copies = [pltpu.make_async_copy(*copy, sem.at[at]) for at, copy in enumerate(copies)]
    for copy in copies:
        copy.start()
    size = edge0.shape[0] // (2 * PARTS)
    for half, edge in enumerate((edge0, edge1)):

        @pl.when(core == half)
        def _():
            extra = []
            for kind, buf in enumerate((q_buf, g_buf)):
                for part in range(PARTS):
                    block = edge.at[pl.ds((kind * PARTS + part) * size, size)]
                    to = buf.at[part, pl.ds(2 * WIDE, size)]
                    extra.append(pltpu.make_async_copy(block, to, sem.at[len(copies) + len(extra)]))
            for copy in extra:
                copy.start()
            for copy in extra:
                copy.wait()

    for copy in copies:
        copy.wait()


def doc_start(pos, len_ref):
    start = jnp.zeros_like(pos)
    end = jnp.int32(0)
    for doc in range(len_ref.shape[0]):
        end = end + len_ref[doc]
        start = jnp.where(end <= pos, end, start)
    return start


def bias_of(first_key, keys, query_pos, start):
    key_pos = first_key + lax.broadcasted_iota(jnp.int32, (keys, query_pos.shape[1]), 0)
    return jnp.where((key_pos >= start) & (key_pos <= query_pos), 0.0, MASKED)


def raise_scores(key, query, bias):
    return lax.dot_general(key, query, NT, preferred_element_type=F32) + bias


def softmax(scores, keep):
    top = jnp.max(scores, axis=0, keepdims=True)
    raw = jnp.exp2((scores - top) * (HD**-0.5 * math.log2(math.e)))
    return raw * (keep / jnp.sum(raw, axis=0, keepdims=True))


def grad_kernel(stage, halo, len_ref, q_buf, g_buf, *refs):
    if stage:
        dk_last, dv_last, *refs = refs
    *got, edge_a, edge_b, dk_ref, dv_ref, k_buf, v_buf = refs
    rows = got[0].shape[0]
    span = GROUP * rows
    me, rank, _ = place()
    first = (me - rank) * rows
    docs = len_ref.shape[0]

    def load(part, blocks):
        here = pl.ds(part * 2 * HD, 2 * HD)
        low, high = jnp.where(rank < 2, edge_a[:, here], edge_b[:, here]), edge_b[:, here]
        for buf, kind in ((k_buf, 0), (v_buf, HD)):
            for step, block in enumerate(blocks):
                at = pl.ds(pl.multiple_of(halo + (rank ^ step) * rows, 16), rows)
                buf[part, at, :] = block[:, kind : kind + HD]
            buf[part, :halo, :] = low[:, kind : kind + HD]
            buf[part, halo + span :, :] = high[:, kind : kind + HD]

    own, one, two, three = got[:4]
    here = pl.ds(stage * 2 * HD, 2 * HD)
    load(stage, (own[...], one[:, here], two[...], three[...]))
    if stage:
        dk_ref[...] = dk_last[...]
        dv_ref[...] = dv_last[...]
    else:
        for part, own in enumerate(got[4:], 1):
            load(part, (own[...], one[:, pl.ds(part * 2 * HD, 2 * HD)]))
        dk_ref[...] = jnp.zeros_like(dk_ref)
        dv_ref[...] = jnp.zeros_like(dv_ref)

    for chip in range(2):

        @pl.when(rank // 2 == chip)
        def _():
            tiles = []
            for part in (stage,) if chip else range(0 if stage == 0 else PARTS, PARTS):
                for slot in range(2):
                    block = 2 * chip + slot
                    query_pos = first + block * rows + lax.broadcasted_iota(jnp.int32, (1, rows), 1)
                    start = doc_start(query_pos, len_ref)
                    keep = jnp.where(start < first - halo, 0.0, 1.0)
                    tiles.append((part, pl.ds(slot * WIDE, WIDE), 0, halo + (block + 1) * rows, query_pos, start, keep, SHARE))
            if chip == 0:
                size = edge_rows(docs)
                lane = lax.broadcasted_iota(jnp.int32, (1, size), 1)
                query_pos = first + span + lax.rem(lane, docs)
                start = doc_start(query_pos, len_ref)
                keep = jnp.where((start < first + span - halo) & (lane < SHARE * docs), 1.0, 0.0)
                tiles.append((stage, pl.ds(2 * WIDE, size), halo, halo + span + halo, query_pos, start, keep, 1))
            def raised(tile):
                part, cols, low, high, query_pos, start, keep, times = tile
                bias = bias_of(first - halo + low, high - low, query_pos, start)
                bias = jnp.concatenate([bias] * times, axis=1)
                return raise_scores(k_buf[part, pl.ds(low, high - low), :], q_buf[part, cols, :], bias)

            tiles.reverse()
            scores = raised(tiles[0])
            for at, (part, cols, low, high, query_pos, start, keep, times) in enumerate(tiles):
                keys = pl.ds(low, high - low)
                query, cot = q_buf[part, cols, :], g_buf[part, cols, :]
                weights = softmax(scores, jnp.concatenate([keep] * times, axis=1))
                if at + 1 < len(tiles):
                    scores = raised(tiles[at + 1])
                dweights = lax.dot_general(v_buf[part, keys, :], cot, NT, preferred_element_type=F32)
                dv_ref[part, keys, :] += lax.dot_general(weights.astype(BF16), cot, NN, preferred_element_type=F32)
                delta = jnp.sum(weights * dweights, axis=0, keepdims=True)
                dscores = (weights * (dweights - delta)).astype(BF16)
                dk_ref[part, keys, :] += lax.dot_general(dscores, query, NN, preferred_element_type=F32)


def terms(dk_ref, dv_ref, part, row, size):
    at = pl.ds(row if isinstance(row, int) else pl.multiple_of(row, 16), size)
    return jnp.concatenate([dk_ref[part, at, :] * HD**-0.5, dv_ref[part, at, :]], axis=1)


def across_kernel(part, halo, dk_ref, dv_ref, across):
    _, rank, _ = place()
    kv = 2 * HD
    rows = across.shape[0] - (0 if part else halo)
    for which in range(PARTS):
        cols = pl.ds(which * kv, kv)
        across[:rows, cols] = terms(dk_ref, dv_ref, part, halo + (rank ^ (2 + which)) * rows, rows).astype(BF16)
        if not part:
            across[rows:, cols] = terms(dk_ref, dv_ref, which, 0, halo).astype(BF16)


def ends_kernel(halo, dk_ref, dv_ref, across, ends):
    _, rank, _ = place()
    kv = 2 * HD
    rows = across.shape[0] - halo
    for part in range(PARTS):
        cols = pl.ds(part * kv, kv)
        before = terms(dk_ref, dv_ref, part, 0, halo) + across[rows:, cols].astype(F32)
        behind = terms(dk_ref, dv_ref, part, halo + GROUP * rows, halo)
        ends[:, cols] = jnp.where(rank < 2, behind, before).astype(BF16)


def join_kernel(dk_ref, dv_ref, across0, across1, ends, mine, other):
    kv = 2 * HD
    halo, (rows, _) = ends.shape[0], mine.shape
    _, rank, _ = place()
    for ref, step, first, last in ((mine, 0, 0, GROUP - 1), (other, 1, 1, GROUP - 2)):
        for part, across in enumerate((across0, across1)):
            cols = pl.ds(part * kv, kv)
            total = terms(dk_ref, dv_ref, part, halo + (rank ^ step) * rows, rows)
            total = total + across[:rows, pl.ds(step * kv, kv)].astype(F32)
            end = ends[:, cols].astype(F32)
            low = total[:halo] + jnp.where(rank == first, end, 0.0)
            high = total[rows - halo :] + jnp.where(rank == last, end, 0.0)
            ref[:, cols] = jnp.concatenate([low, total[halo : rows - halo], high], axis=0).astype(ref.dtype)


def grads(stage, halo, rows, *inputs):
    total = (PARTS, halo + GROUP * rows + halo, HD)
    vmem = pl.BlockSpec(memory_space=pltpu.VMEM)
    return call(
        functools.partial(grad_kernel, stage, halo),
        [jax.ShapeDtypeStruct(total, F32)] * 2,
        in_specs=[pl.BlockSpec(memory_space=pltpu.SMEM)] + [vmem] * (len(inputs) - 1),
        scratch_shapes=[pltpu.VMEM(total, BF16)] * 2,
        mib=24,
        flops=COST,
    )(*inputs)


COST = 4 * 10**9


def place_kernel(other, block, *refs):
    *_, out_ref, heads, sem = refs
    _, _, core = place()
    half = 1 - core if other else core
    copies = []
    for kind in range(2):
        for part in range(PARTS):
            to = (kind * PARTS + part) * HD
            heads[:, to : to + HD] = block[:, pl.ds((part * 2 + kind) * HD, HD)].astype(BF16)
        wide = PARTS * HD
        to = pl.ds(pl.multiple_of((kind * KVH + half * PARTS) * HD, HD), wide)
        copies.append(pltpu.make_async_copy(heads.at[:, pl.ds(kind * wide, wide)], out_ref.at[0, :, to], sem.at[kind]))
        copies[-1].start()
    for copy in copies:
        copy.wait()


def on_device(queries, stash, grad_out, lengths):
    rows = queries.shape[1]
    pipe, ctx = lax.axis_size("pipe"), lax.axis_size("ctx")
    halo = -(-lengths.shape[0] // 16) * 16
    high = 1 << (pipe.bit_length() - 2)

    def pairs(pick):
        return [(c, (c + pick[c % GROUP]) % ctx) for c in range(ctx)]

    def partner(block, pick):
        route = [((p ^ high) * ctx + c, p * ctx + d) for p in range(pipe) for c, d in pairs(pick)]
        return lax.ppermute(block, ("pipe", "ctx"), route)

    def along(block, pick):
        return lax.ppermute(block, "ctx", pairs(pick))

    stay = (0,) * GROUP
    flip = [tuple((rank ^ step) - rank for rank in range(GROUP)) for step in range(GROUP)]

    def shape(*dims):
        return jax.ShapeDtypeStruct(dims, BF16)

    def after(value, *others):
        return lax.optimization_barrier((value, *others))[0]

    edge_wide = 2 * PARTS * HD
    hbm = pl.BlockSpec(memory_space=pltpu.HBM)
    held = partner(stash, stay)

    wide = PARTS * WIDE
    size = edge_rows(lengths.shape[0])

    def beside(queries, grad_out):
        far, edge0, edge1 = call(
            functools.partial(hand_kernel, halo, lengths.shape[0]),
            [shape(2 * rows, wide), *[shape(2 * PARTS * size, HD)] * 2],
            in_specs=[hbm] * 2,
            scratch_shapes=[pltpu.VMEM((halo, 2 * wide), BF16)] * 2 + [pltpu.SemaphoreType.DMA((4,))],
        )(queries, grad_out)
        return along(far, flip[1]), along(edge0, (-4, -4, 4, 4)), along(edge1, (-3, -5, 5, 3))

    def nothing(*_):
        return jnp.zeros((2 * rows, wide), BF16), *[jnp.zeros((2 * PARTS * size, HD), BF16)] * 2

    far, edge0, edge1 = lax.cond(lengths[0] > 0, beside, nothing, queries, grad_out)
    q_buf, g_buf = call(
        stage_kernel,
        [shape(PARTS, 2 * WIDE + size, HD)] * 2,
        in_specs=[hbm] * 5,
        scratch_shapes=[pltpu.SemaphoreType.DMA((4 * PARTS * SHARE + 2 * PARTS,))],
    )(queries, grad_out, far, edge0, edge1)
    held, q_buf, g_buf = lax.optimization_barrier((held, q_buf, g_buf))
    far, *parts = call(split_kernel, [shape(rows, edge_wide), *[shape(rows, 2 * HD)] * (2 * PARTS)])(held)
    owns, fars = parts[:PARTS], parts[PARTS:]

    one = along(far, flip[1])
    got = [(own, one, along(own, flip[2]), along(far, flip[3])) for own, far in zip(owns, fars)]
    edge = call(edge_kernel, shape(halo, edge_wide))(*owns, one)
    edges = along(edge, (2, 2, 2, 2)), along(edge, (-4, -4, 4, 4))
    raw = grads(0, halo, rows, lengths, q_buf, g_buf, *got[0], *owns[1:], *edges)
    first = call(functools.partial(across_kernel, 0, halo), shape(rows + halo, edge_wide))(*raw)
    first = along(first, flip[2])
    raw = grads(1, halo, rows, lengths, q_buf, g_buf, *raw, *got[1], *edges)
    second = along(call(functools.partial(across_kernel, 1, halo), shape(rows, edge_wide))(*raw), flip[2])
    ends = along(call(functools.partial(ends_kernel, halo), shape(halo, edge_wide))(*raw, first), (4, 4, -4, -4))
    mine, other = call(
        join_kernel, [jax.ShapeDtypeStruct((rows, edge_wide), F32), shape(rows, edge_wide)]
    )(*raw, first, second, ends)
    vmem = pl.BlockSpec(memory_space=pltpu.VMEM)
    settle = dict(
        out=shape(1, rows, 2 * KVH * HD),
        out_specs=hbm,
        scratch_shapes=[pltpu.VMEM((rows, edge_wide), BF16), pltpu.SemaphoreType.DMA((2,))],
    )
    out = call(functools.partial(place_kernel, False), in_specs=[vmem], **settle)(mine)
    return call(
        functools.partial(place_kernel, True), in_specs=[vmem, hbm], input_output_aliases={1: 0}, **settle
    )(along(other, flip[1]), out)


def solution(mesh):
    placed = (P("pipe", "ctx", None), P("pipe", "ctx", None), P("pipe", "ctx", None), P())
    return jax.shard_map(
        on_device, mesh=mesh, in_specs=placed, out_specs=P("pipe", "ctx", None), check_vma=False
    )
```
